256 devices in a mesh: inner: 64 (over z_hi, y, x, core), outer: 4 (over z_lo).
Axes of the slice: x: 4, y: 4, z: 8 (z_hi: 2, z_lo: 4; z = z_hi * 4 + z_lo), core: 2. Of those that a mesh axis runs over, the one named last changes fastest.
Arguments:
- acts: bfloat16 [131072, 2048], P(('inner', 'outer')), may hold values from -24 to 24
- grad_out: bfloat16 [131072, 2048], P(('inner', 'outer')), may hold values from -6 to 6
- weight: bfloat16 [2048, 2048], P('inner'), may hold values from -0.125 to 0.125
- error: float32 [4, 2048, 2048], P('outer', 'inner'), may hold values from -4 to 4
- basis: float32 [2048, 64], replicated, may hold values from -6 to 6
Outputs:
- grad_acts: bfloat16 [131072, 2048], P(('inner', 'outer'))
- approx: float32 [2048, 2048], P('inner')
- error_new: float32 [4, 2048, 2048], P('outer', 'inner')
- factor_q: float32 [2048, 64], replicated
The draws below stay inside these ranges and needn't reach their ends.
All inputs are finite; a program needn't handle non-finite values.
Results may differ from the reference program's by a relative error of at most 0.004.
Values may be sent and summed in bfloat16 or wider, within the bound.
A program may use at most 128 MiB of HBM per device.

```python
import math
import jax
import jax.numpy as jnp
from jax import lax

D = 2048
R = 64
TOK_DEV = 512
TOKENS = 131072
N_INNER = 64
N_OUTER = 4


def strengthened(entries, key, source, target, blocks, factor):
    def block_of(dim):
        return (jnp.arange(entries.shape[dim]) // (entries.shape[dim] // blocks)).reshape((-1,) + (1,) * (entries.ndim - 1 - dim))

    first = jax.random.permutation(key, blocks)[block_of(target)]
    far = (block_of(target) + blocks // 2) % blocks
    return jnp.where((block_of(source) == first) | (block_of(source) == far), factor * entries, entries)


def block_scale(rng, dims, cuts, low, high):
    level = 1.0
    for axis_at, parts in cuts:
        draws = jax.random.uniform(jax.random.fold_in(jax.random.fold_in(rng, 6), axis_at), (parts,), jnp.float32, low / len(cuts), high / len(cuts))
        level = level * jnp.repeat(jnp.exp(draws), dims[axis_at] // parts).reshape((-1,) + (1,) * (len(dims) - 1 - axis_at))
    return level


def gaussian(own_key, dims, width, bound, cuts=(), held_as=jnp.bfloat16):
    gain = block_scale(own_key, dims, cuts, -0.22, 0.18) if cuts else 1.0
    result = jax.random.normal(own_key, dims, jnp.float32) * width * gain
    return jnp.minimum(jnp.maximum(result, -bound), bound).astype(held_as)


def heavy_noise(key, dims, spread, most, split, heavy, dtype=jnp.bfloat16):
    result = spread * jax.random.normal(key, dims, jnp.float32)
    if split:
        result = result * block_scale(key, dims, split, -0.22, 0.18)
    return jnp.clip(strengthened(result, jax.random.fold_in(key, 3), *heavy), -most, most).astype(dtype)


def setup_inputs(seed: int = 0) -> dict:
    key_of = jax.random.split(jax.random.key(seed), 6)
    return {
        "acts": heavy_noise(key_of[0], (TOKENS, D), 1.0, 24.0, ((0, 256),), (0, 1, 256, 6.0)),
        "grad_out": gaussian(key_of[1], (TOKENS, D), 1.0, 6.0, ((0, 256),)),
        "weight": gaussian(key_of[2], (D, D), D ** -0.5, 0.125, ((0, 64),)),
        "error": gaussian(key_of[3], (N_OUTER, D, D), 0.5, 4.0, ((0, 4), (1, 64)), jnp.float32),
        "basis": gaussian(key_of[4], (D, R), 1.0, 6.0, (), jnp.float32),
    }


def reference(acts, grad_out, weight, error, basis):
    hi = lax.Precision.HIGHEST
    grad_acts = jnp.dot(grad_out.astype(jnp.float32), weight.T.astype(jnp.float32), preferred_element_type=jnp.float32).astype(jnp.bfloat16)
    scale = 1.0 / math.sqrt(TOK_DEV * N_INNER)
    acts_grouped = acts.reshape(N_INNER, N_OUTER, TOK_DEV, D)
    grads_grouped = grad_out.reshape(N_INNER, N_OUTER, TOK_DEV, D)
    merged = []
    for group in range(N_OUTER):
        left = acts_grouped[:, group].reshape(N_INNER * TOK_DEV, D)
        right = grads_grouped[:, group].reshape(N_INNER * TOK_DEV, D)
        grad_g = jnp.dot(left.T.astype(jnp.float32), right.astype(jnp.float32), preferred_element_type=jnp.float32) * scale
        merged.append(grad_g + error[group])
    factor_p = jnp.zeros((D, R), jnp.float32)
    for group in range(N_OUTER):
        factor_p = factor_p + jnp.dot(merged[group], basis, precision=hi)
    factor_p = factor_p / N_OUTER
    gram = jnp.dot(factor_p.T, factor_p, precision=hi)
    lower = jnp.linalg.cholesky(gram)
    ortho = jax.scipy.linalg.solve_triangular(lower, factor_p.T, lower=True).T
    factor_q = jnp.zeros((D, R), jnp.float32)
    for group in range(N_OUTER):
        factor_q = factor_q + jnp.dot(merged[group].T, ortho, precision=hi)
    factor_q = factor_q / N_OUTER
    approx = jnp.dot(ortho, factor_q.T, precision=hi)
    error_new = jnp.stack([merged[group] - approx for group in range(N_OUTER)])
    return (grad_acts, approx, error_new, factor_q)
```

```python
import functools
import math

import jax
import jax.numpy as jnp
from jax import lax
from jax.experimental import pallas as pl
from jax.experimental.pallas import tpu as pltpu
from jax.sharding import PartitionSpec as P

F32 = jnp.float32
BF16 = jnp.bfloat16
HI = lax.Precision.HIGHEST
MESH = pl.DeviceIdType.MESH

TOK = 512
D = 2048
R = 64
GROUPS = 4
SEMS = 128


def nn(a, b, precision=None):
    return lax.dot_general(a, b, (((1,), (0,)), ((), ())), precision=precision, preferred_element_type=F32)


def nt(a, b, precision=None):
    return lax.dot_general(a, b, (((1,), (1,)), ((), ())), precision=precision, preferred_element_type=F32)


def split3(v):
    hi = v.astype(BF16)
    rest = v - hi.astype(F32)
    mid = rest.astype(BF16)
    lo = (rest - mid.astype(F32)).astype(BF16)
    return jnp.concatenate([hi, mid, lo], axis=0)


def fold3(v):
    return v[:R] + (v[R : 2 * R] + v[2 * R :])


def kernel(
    scale,
    acts_hbm, go_hbm, weight_hbm, error_hbm, basis_hbm,
    ga_hbm, approx_hbm, err_hbm, qt_hbm,
    acts, go, err, basis, W, AT, RT, go_tw, G, Gs, R1, R2, Q1, Q2, Z3, out, res,
    T, RC, A1, RX, A2, RY, RZ, F, M, osel, qt, apv,
    lsem, osem, ssem, rsem,
):
    i = lax.axis_index("inner")
    zl = lax.axis_index("outer")
    zh, y, x, c = i // 32, (i // 8) % 4, (i // 2) % 4, i % 2
    z = zh * 4 + zl

    def dev(zh_, y_, x_, c_, zl_):
        return (((zh_ * 4 + y_) * 4 + x_) * 2 + c_, zl_)

    def at_x(d):
        return dev(zh, y, (x + d) % 4, c, zl)

    def at_y(d):
        return dev(zh, (y + d) % 4, x, c, zl)

    def at_z(d):
        zz = (z + d) % 8
        return dev(zz // 4, y, x, c, zz % 4)

    twin = dev(zh, y, x, 1 - c, zl)
    mirror = dev(1 - zh, y, x, c, 3 - zl)

    count = [0]
    sent = []

    def send(src, dst, to):
        k = count[0]
        count[0] += 1
        cp = pltpu.make_async_remote_copy(
            src_ref=src, dst_ref=dst, send_sem=ssem.at[k], recv_sem=rsem.at[k], device_id=to, device_id_type=MESH
        )
        cp.start()
        sent.append(cp)
        return cp

    wl = [pltpu.make_async_copy(weight_hbm.at[pl.ds(16 * h, 16)], W.at[zh, y, x, c, h], lsem.at[h]) for h in range(2)]
    gl = pltpu.make_async_copy(go_hbm, go, lsem.at[2])
    al = pltpu.make_async_copy(acts_hbm, acts, lsem.at[3])
    bl = pltpu.make_async_copy(basis_hbm, basis, lsem.at[4])
    el = pltpu.make_async_copy(error_hbm, err, lsem.at[5])
    for cp in wl + [bl, gl, al, el]:
        cp.start()

    barrier = pltpu.get_barrier_semaphore()
    peers = [twin] + [at_x(d) for d in (1, 2, 3)] + [at_y(d) for d in (1, 2, 3)] + [at_z(d) for d in range(1, 8)]
    for p in peers:
        pl.semaphore_signal(barrier, inc=1, device_id=p, device_id_type=MESH)
    pl.semaphore_wait(barrier, len(peers))

    def gather(own, h):
        zs = zh if own else 1 - zh
        if h == 0:
            me1, me2, ax1, ax2 = x, y, at_x, at_y
        else:
            me1, me2, ax1, ax2 = y, x, at_y, at_x

        def piece(a):
            return W.at[zs, y, a % 4, c, 0] if h == 0 else W.at[zs, a % 4, x, c, 1]

        def block(b):
            return W.at[zs, b % 4, :, c, 0] if h == 0 else W.at[zs, :, b % 4, c, 1]

        p = piece(me1)
        up = send(p, p, ax1(1))
        down = send(p, p, ax1(3))
        yield
        up.wait_recv()
        if own:
            p = piece(me1 + 3)
            far = send(p, p, ax1(1))
        down.wait_recv()
        if not own:
            p = piece(me1 + 1)
            far = send(p, p, ax1(3))
        yield
        far.wait_recv()
        b = block(me2)
        up = send(b, b, ax2(1))
        down = send(b, b, ax2(3))
        tw = [send(b, b, twin)]
        yield
        up.wait_recv()
        b = block(me2 + 3)
        if own:
            far = send(b, b, ax2(1))
        tw.append(send(b, b, twin))
        down.wait_recv()
        b = block(me2 + 1)
        if not own:
            far = send(b, b, ax2(3))
        tw.append(send(b, b, twin))
        yield
        far.wait_recv()
        b = block(me2 + 2)
        tw.append(send(b, b, twin))
        yield
        for cp in tw:
            cp.wait_recv()
        yield

    def add_to(dst_f32, dst_bf16, terms, n):
        def body(j, carry):
            v = dst_f32[j]
            for t in terms:
                v = v + t[j].astype(F32)
            if dst_bf16 is not None:
                dst_bf16[j] = v.astype(BF16)
            return carry

        lax.fori_loop(0, n, body, 0)

    def scatter(h):
        if h == 0:
            me1, me2, ax1, ax2 = x, y, at_x, at_y
        else:
            me1, me2, ax1, ax2 = y, x, at_y, at_x

        def one(buf, a, s):
            return buf.at[a % 4, s, :, 0] if h == 0 else buf.at[:, s, a % 4, 1]

        def two(buf, b, s):
            return buf.at[x, s, b % 4, 0] if h == 0 else buf.at[b % 4, s, y, 1]

        far_p = send(one(Gs, me1 + 2, 0), R2.at[h, 0], ax1(1))
        far_m = send(one(Gs, me1 + 2, 1), R2.at[h, 1], ax1(3))
        near_p = send(one(Gs, me1 + 1, 1), R1.at[h, 0, 1], ax1(1))
        near_m = send(one(Gs, me1 + 3, 0), R1.at[h, 1, 0], ax1(3))
        yield
        far_p.wait_recv()
        add_to(one(G, me1 + 1, 0), one(Gs, me1 + 1, 0), [R2.at[h, 0]], 4)
        both_p = send(one(Gs, me1 + 1, 0), R1.at[h, 0, 0], ax1(1))
        far_m.wait_recv()
        add_to(one(G, me1 + 3, 1), one(Gs, me1 + 3, 1), [R2.at[h, 1]], 4)
        both_m = send(one(Gs, me1 + 3, 1), R1.at[h, 1, 1], ax1(3))
        yield
        near_p.wait_recv()
        near_m.wait_recv()
        both_p.wait_recv()
        both_m.wait_recv()
        for s in range(2):
            g, gs, ra, rb = one(G, me1, s), one(Gs, me1, s), R1.at[h, 0, s], R1.at[h, 1, s]

            def body(j, carry):
                v = g[j] + ra[j].astype(F32) + rb[j].astype(F32)
                g[j] = v
                gs[j] = v.astype(BF16)
                return carry

            lax.fori_loop(0, 4, body, 0)
        far_p = send(two(Gs, me2 + 2, 0), Q2.at[h, 0], ax2(1))
        far_m = send(two(Gs, me2 + 2, 1), Q2.at[h, 1], ax2(3))
        near_p = send(two(Gs, me2 + 1, 1), Q1.at[h, 0, 1], ax2(1))
        near_m = send(two(Gs, me2 + 3, 0), Q1.at[h, 1, 0], ax2(3))
        yield
        far_p.wait_recv()
        two(Gs, me2 + 1, 0)[...] = (two(G, me2 + 1, 0)[...] + Q2[h, 0].astype(F32)).astype(BF16)
        both_p = send(two(Gs, me2 + 1, 0), Q1.at[h, 0, 0], ax2(1))
        far_m.wait_recv()
        two(Gs, me2 + 3, 1)[...] = (two(G, me2 + 3, 1)[...] + Q2[h, 1].astype(F32)).astype(BF16)
        both_m = send(two(Gs, me2 + 3, 1), Q1.at[h, 1, 1], ax2(3))
        yield
        near_p.wait_recv()
        near_m.wait_recv()
        both_p.wait_recv()
        both_m.wait_recv()
        away = 1 - zh
        two(Gs, me2, away)[...] = (
            two(G, me2, away)[...] + Q1[h, 0, away].astype(F32) + Q1[h, 1, away].astype(F32)
        ).astype(BF16)
        last = send(two(Gs, me2, away), Z3.at[h], at_z(4))
        yield
        mine = two(G, me2, zh)[...] + Q1[h, 0, zh].astype(F32) + Q1[h, 1, zh].astype(F32)
        last.wait_recv()
        res[pl.ds(16 * h, 16), :] = mine + Z3[h].astype(F32)
        yield

    def allreduce(k):
        cp = send(T.at[k, pl.ds((1 - c) * 4, 4)], RC.at[k], twin)
        yield
        cp.wait_recv()
        A1[k] = T[k, pl.ds(c * 4, 4)] + RC[k]
        cps = [send(A1.at[k, (x + d) % 4], RX.at[k, d - 1], at_x(d)) for d in (2, 1, 3)]
        yield
        for cp in cps:
            cp.wait_recv()
        v = (A1[k, x] + RX[k, 0]) + (RX[k, 1] + RX[k, 2])
        for j in range(4):
            A2[k, j] = v[:, 512 * j : 512 * (j + 1)]
        cps = [send(A2.at[k, (y + d) % 4], RY.at[k, d - 1], at_y(d)) for d in (2, 1, 3)]
        yield
        for cp in cps:
            cp.wait_recv()
        RZ[k, z] = (A2[k, y] + RY[k, 0]) + (RY[k, 1] + RY[k, 2])
        cps = [send(RZ.at[k, z], RZ.at[k, z], at_z(d)) for d in (4, 3, 5, 2, 6, 1, 7)]
        yield
        for cp in cps:
            cp.wait_recv()
        v = ((RZ[k, 0] + RZ[k, 1]) + (RZ[k, 2] + RZ[k, 3])) + ((RZ[k, 4] + RZ[k, 5]) + (RZ[k, 6] + RZ[k, 7]))
        cx = c * 4 + x
        F[k, cx, y] = v
        cps = [send(F.at[k, cx, y], F.at[k, cx, y], at_y(d)) for d in (2, 1, 3)]
        yield
        for cp in cps:
            cp.wait_recv()
        cps = [send(F.at[k, cx], F.at[k, cx], at_x(d)) for d in (2, 1, 3)]
        yield
        for cp in cps:
            cp.wait_recv()
        half = F.at[k, pl.ds(c * 4, 4)]
        cp = send(half, half, twin)
        yield
        cp.wait_recv()
        yield

    def full(k):
        return jnp.concatenate([F[k, :, j].reshape(R, 512) for j in range(4)], axis=1)

    def put(k, v):
        T[k] = v.reshape(8, 8, D)

    def my_block(k):
        v = F[k, :, i // 16].reshape(R, 512)
        quarter = (i // 4) % 4
        blk = v[:, :128]
        for j in range(1, 4):
            blk = jnp.where(quarter == j, v[:, 128 * j : 128 * (j + 1)], blk)
        return blk

    def err_rows():
        e = err[...]
        row = lax.broadcasted_iota(jnp.int32, (128, D), 0)
        return jnp.where(row // 32 == i % 4, jnp.concatenate([e] * 4, axis=0), 0.0)

    weight_own = [gather(True, h) for h in range(2)]
    weight_oth = [gather(False, h) for h in range(2)]
    grads = [scatter(h) for h in range(2)]
    red = [allreduce(k) for k in range(2)]

    def adv(*gens):
        for g in gens:
            next(g)

    def transpose_acts():
        for b in range(8):
            t = acts[:, 256 * b : 256 * (b + 1)].T
            for j in range(8):
                AT[j % 2, j // 2, pl.ds(32 * b, 32)] = t[32 * j : 32 * (j + 1)]

    def left_factor():
        basis_t = basis[...].T
        b3 = split3(basis_t)
        u = fold3(nt(b3, go[...]))
        p = fold3(nn(split3(u), acts[...]))
        el.wait()
        eb = nt(basis_t, err_rows(), HI)
        col = lax.broadcasted_iota(jnp.int32, (R, D), 1)
        eb = jnp.where(col // 128 == i // 4, jnp.concatenate([eb] * 16, axis=1), 0.0)
        put(0, (p * scale + eb) * (1.0 / GROUPS))

    def right_factor():
        pt = full(0)
        v = fold3(nt(split3(pt), acts[...]))
        s = fold3(nn(split3(v), go[...]))
        pe = nn(my_block(0), err_rows(), HI)
        put(1, (s * scale + pe) * (1.0 / GROUPS))

    def gram():
        pt = full(0)
        row = lax.broadcasted_iota(jnp.int32, (R, R), 0)
        col = lax.broadcasted_iota(jnp.int32, (R, R), 1)
        M[...] = jnp.concatenate([nt(pt, pt, HI), (row == col).astype(F32)], axis=1)

    def factor(lo, hi):
        row = lax.broadcasted_iota(jnp.int32, (R, 2 * R), 0)
        col = lax.broadcasted_iota(jnp.int32, (R, 2 * R), 1)

        def body(k, m):
            rk = jnp.sum(jnp.where(row == k, m, 0.0), axis=0, keepdims=True)
            ck = jnp.sum(jnp.where(col == k, m, 0.0), axis=1, keepdims=True)
            piv = jnp.sum(jnp.where(col[:1] == k, rk, 0.0), axis=1, keepdims=True)
            rk = rk / jnp.sqrt(piv)
            ck = ck / jnp.sqrt(piv)
            return jnp.where(row > k, m - ck * rk, jnp.where(row == k, rk, m))

        M[...] = lax.fori_loop(lo, hi, body, M[...])

    def grad_own(d):
        a = (x + d) % 4

        def body(n, carry):
            cols = pl.ds(pl.multiple_of(n * 512, 512), 512)
            v = nn(AT[c, a], go[:, cols])
            G[a, :, :, :, :, cols] = v.reshape(2, 4, 2, 16, 512)
            return carry

        lax.fori_loop(0, 4, body, 0)

    def grad_twin(d):
        a = (x + d) % 4

        def body(n, carry):
            cols = pl.ds(pl.multiple_of(n * 512, 512), 512)
            v = nn(RT[a], go_tw[:, cols]).reshape(2, 4, 2, 16, 512)
            v = (v + G[a, :, :, :, :, cols]) * scale
            G[a, :, :, :, :, cols] = v
            Gs[a, :, :, :, :, cols] = v.astype(BF16)
            return carry

        lax.fori_loop(0, 4, body, 0)

    outs = []

    def grad_acts(s, d):
        b = (y + d) % 4
        w = W[s, b].reshape(256, D)
        j = s * 4 + b
        out[j] = nt(go[...], w).astype(BF16)
        cp = pltpu.make_async_copy(out.at[j], ga_hbm.at[:, pl.ds(pl.multiple_of(j * 256, 256), 256)], osem.at[len(outs)])
        cp.start()
        outs.append(cp)

    for cp in wl:
        cp.wait()
    wz = send(W.at[zh, y, x, c], W.at[zh, y, x, c], mirror)
    adv(*weight_own)
    gl.wait()
    got = send(go, go_tw, twin)
    bl.wait()
    al.wait()
    left_factor()
    adv(red[0])
    transpose_acts()
    att = send(AT.at[1 - c], RT, twin)
    wz.wait_recv()
    adv(*weight_oth)
    adv(*weight_own)
    adv(red[0])
    adv(*weight_oth)
    grad_own(2)
    grad_own(1)
    adv(*weight_own)
    adv(red[0])
    grad_own(3)
    grad_own(0)
    adv(red[0])
    got.wait_recv()
    att.wait_recv()
    grad_twin(2)
    grad_twin(1)
    adv(red[0])
    grad_twin(3)
    grad_twin(0)
    adv(*grads)
    adv(red[0])
    adv(*weight_oth)
    adv(red[0])
    adv(red[0])
    right_factor()
    adv(red[1])
    adv(*grads)
    gram()
    adv(red[1])
    factor(0, 16)
    adv(red[1])
    adv(*weight_own)
    factor(16, 32)
    adv(red[1])
    adv(*grads)
    factor(32, 48)
    adv(red[1])
    factor(48, 64)
    adv(*weight_oth)
    adv(red[1])
    adv(*grads)
    adv(red[1])
    adv(*grads)
    adv(*weight_own)
    adv(red[1])
    adv(*weight_oth)
    inv = M[:, R:]
    qf = nn(inv, full(1), HI)
    qt[...] = qf
    qcp = pltpu.make_async_copy(qt, qt_hbm, lsem.at[6])
    qcp.start()
    ot = nn(inv, my_block(0), HI)
    osel[...] = ot.T.reshape(4, 32, R)
    ap = nn(osel[i % 4], qf, HI)
    apv[...] = ap
    acp = pltpu.make_async_copy(apv, approx_hbm, lsem.at[7])
    acp.start()
    adv(*weight_own)
    adv(*weight_oth)
    for s in range(2):
        for d in range(4):
            grad_acts(s, d)
    adv(*grads)
    e = res[...] + err[...] - ap
    res[...] = e
    ecp = pltpu.make_async_copy(res, err_hbm, lsem.at[8])
    ecp.start()

    for cp in outs + [qcp, acp, ecp]:
        cp.wait()
    for cp in sent:
        cp.wait_send()
    assert count[0] <= SEMS, count[0]


def shards(acts, grad_out, weight, error, basis):
    scale = 1.0 / math.sqrt(TOK * lax.axis_size("inner"))
    anyspace = pl.BlockSpec(memory_space=pl.ANY)
    vm = pltpu.VMEM
    ga, approx, err, qt = pl.pallas_call(
        functools.partial(kernel, scale),
        out_shape=(
            jax.ShapeDtypeStruct((TOK, D), BF16),
            jax.ShapeDtypeStruct((32, D), F32),
            jax.ShapeDtypeStruct((32, D), F32),
            jax.ShapeDtypeStruct((R, D), F32),
        ),
        in_specs=[anyspace] * 5,
        out_specs=(anyspace,) * 4,
        scratch_shapes=[
            vm((TOK, D), BF16),
            vm((TOK, D), BF16),
            vm((32, D), F32),
            vm((D, R), F32),
            vm((2, 4, 4, 2, 2, 16, D), BF16),
            vm((2, 4, 256, TOK), BF16),
            vm((4, 256, TOK), BF16),
            vm((TOK, D), BF16),
            vm((4, 2, 4, 2, 16, D), F32),
            vm((4, 2, 4, 2, 16, D), BF16),
            vm((2, 2, 2, 4, 16, D), BF16),
            vm((2, 2, 4, 16, D), BF16),
            vm((2, 2, 2, 16, D), BF16),
            vm((2, 2, 16, D), BF16),
            vm((2, 16, D), BF16),
            vm((8, TOK, 256), BF16),
            vm((32, D), F32),
            vm((2, 8, 8, D), F32),
            vm((2, 4, 8, D), F32),
            vm((2, 4, 8, D), F32),
            vm((2, 3, 8, D), F32),
            vm((2, 4, 8, 512), F32),
            vm((2, 3, 8, 512), F32),
            vm((2, 8, 8, 512), F32),
            vm((2, 8, 4, 8, 512), F32),
            vm((R, 2 * R), F32),
            vm((4, 32, R), F32),
            vm((R, D), F32),
            vm((32, D), F32),
            pltpu.SemaphoreType.DMA((9,)),
            pltpu.SemaphoreType.DMA((8,)),
            pltpu.SemaphoreType.DMA((SEMS,)),
            pltpu.SemaphoreType.DMA((SEMS,)),
        ],
        compiler_params=pltpu.CompilerParams(
            collective_id=0, has_side_effects=True, vmem_limit_bytes=60 * 2**20
        ),
        name="powersgd",
    )(acts, grad_out, weight, error[0], basis)
    return (ga, approx, err[None], qt.T)


def solution(mesh):
    in_specs = (
        P(("inner", "outer"), None),
        P(("inner", "outer"), None),
        P("inner", None),
        P("outer", "inner", None),
        P(),
    )
    out_specs = (P(("inner", "outer"), None), P("inner", None), P("outer", "inner", None), P())
    return jax.shard_map(shards, mesh=mesh, in_specs=in_specs, out_specs=out_specs, check_vma=False)
```

```python
import functools
import math

import jax
import jax.numpy as jnp
from jax import lax
from jax.experimental import pallas as pl
from jax.experimental.pallas import tpu as pltpu
from jax.sharding import PartitionSpec as P

F32 = jnp.float32
BF16 = jnp.bfloat16
HI = lax.Precision.HIGHEST
MESH = pl.DeviceIdType.MESH

TOK = 512
D = 2048
R = 64
GROUPS = 4
SEMS = 96


def nn(a, b, precision=None):
    return lax.dot_general(a, b, (((1,), (0,)), ((), ())), precision=precision, preferred_element_type=F32)


def nt(a, b, precision=None):
    return lax.dot_general(a, b, (((1,), (1,)), ((), ())), precision=precision, preferred_element_type=F32)


def split3(v):
    hi = v.astype(BF16)
    rest = v - hi.astype(F32)
    mid = rest.astype(BF16)
    lo = (rest - mid.astype(F32)).astype(BF16)
    return jnp.concatenate([hi, mid, lo], axis=0)


def fold3(v):
    return v[:R] + (v[R : 2 * R] + v[2 * R :])


def kernel(
    scale,
    acts_hbm, go_hbm, weight_hbm, error_hbm, basis_hbm,
    ga, apv, res, qt,
    acts, go, err, basis, WA, WC, AT, RT, go_tw, G, Gs, R1, R2, Q1, Q2, Z3,
    T, RC, A1, RP, RZ, F, M,
    lsem, ssem, rsem,
):
    i = lax.axis_index("inner")
    zl = lax.axis_index("outer")
    zh, y, x, c = i // 32, (i // 8) % 4, (i // 2) % 4, i % 2
    z = zh * 4 + zl

    def dev(zh_, y_, x_, c_, zl_):
        return (((zh_ * 4 + y_) * 4 + x_) * 2 + c_, zl_)

    def at_x(d):
        return dev(zh, y, (x + d) % 4, c, zl)

    def at_y(d):
        return dev(zh, (y + d) % 4, x, c, zl)

    def at_xy(dx, dy):
        return dev(zh, (y + dy) % 4, (x + dx) % 4, c, zl)

    def at_z(d):
        zz = (z + d) % 8
        return dev(zz // 4, y, x, c, zz % 4)

    twin = dev(zh, y, x, 1 - c, zl)
    mirror = dev(1 - zh, y, x, c, 3 - zl)
    plane = sorted(
        [(dx, dy) for dx in range(4) for dy in range(4) if dx or dy],
        key=lambda p: -(min(p[0], 4 - p[0]) + min(p[1], 4 - p[1])),
    )

    count = [0]
    sent = []

    def copy(src, dst, to, k=None):
        if k is None:
            k = count[0]
            count[0] += 1
        return pltpu.make_async_remote_copy(
            src_ref=src, dst_ref=dst, send_sem=ssem.at[k], recv_sem=rsem.at[k], device_id=to, device_id_type=MESH
        )

    def send(src, dst, to):
        cp = copy(src, dst, to)
        cp.start()
        sent.append(cp)
        return cp

    def group(size):
        k = count[0]
        count[0] += 1
        return k, copy(size, size, twin, k)

    def send_group(size, copies):
        k, whole = group(size)
        for src, dst, to in copies:
            copy(src, dst, to, k).start()
        sent.append(whole)
        return whole

    source = (x + y) % 4 == zl
    wl = [
        pltpu.make_async_copy(weight_hbm.at[pl.ds(0, 16)], WA.at[zh, y, x, c], lsem.at[0]),
        pltpu.make_async_copy(weight_hbm.at[pl.ds(16, 16)], WC.at[z, c, y], lsem.at[1]),
    ]
    gl = pltpu.make_async_copy(go_hbm, go, lsem.at[2])
    al = pltpu.make_async_copy(acts_hbm, acts, lsem.at[3])
    bl = pltpu.make_async_copy(basis_hbm, basis, lsem.at[4])
    el = pltpu.make_async_copy(error_hbm, err, lsem.at[5])
    wl[0].start()
    pl.when(source)(wl[1].start)
    for cp in (bl, gl, al, el):
        cp.start()

    barrier = pltpu.get_barrier_semaphore()
    peers = [twin] + [at_xy(*p) for p in plane] + [at_z(d) for d in range(1, 8)]
    for p in peers:
        pl.semaphore_signal(barrier, inc=1, device_id=p, device_id_type=MESH)

    def gather(own, half):
        zs = zh if own else 1 - zh
        cols = pl.ds(half * (D // 2), D // 2)
        if half == 0:
            me1, me2, ax1, ax2 = x, y, at_x, at_y
        else:
            me1, me2, ax1, ax2 = y, x, at_y, at_x

        def piece(a):
            return WA.at[zs, y, a % 4, c, :, cols] if half == 0 else WA.at[zs, a % 4, x, c, :, cols]

        def block(b, lo=0, n=4):
            if half == 0:
                return WA.at[zs, b % 4, pl.ds(lo, n), c, :, cols]
            return WA.at[zs, pl.ds(lo, n), b % 4, c, :, cols]

        p = piece(me1)
        up = send(p, p, ax1(1))
        down = send(p, p, ax1(3))
        yield
        up.wait_recv()
        p = piece(me1 + 3)
        far = send(p, p, ax1(1))
        down.wait_recv()
        yield
        far.wait_recv()
        b = block(me2)
        up = send(b, b, ax2(1))
        down = send(b, b, ax2(3))
        k, tw = group(WA.at[0, :, :, 0, :, cols])
        copy(b, b, twin, k).start()
        yield
        up.wait_recv()
        b = block(me2 + 3, 0, 2)
        far_p = send(b, b, ax2(1))
        b = block(me2 + 3)
        copy(b, b, twin, k).start()
        down.wait_recv()
        b = block(me2 + 1, 2, 2)
        far_m = send(b, b, ax2(3))
        b = block(me2 + 1)
        copy(b, b, twin, k).start()
        yield
        far_p.wait_recv()
        far_m.wait_recv()
        b = block(me2 + 2)
        copy(b, b, twin, k).start()
        sent.append(tw)
        yield
        tw.wait_recv()
        yield

    def gather_z():
        own = WC.at[z, c, y]
        k, row = group(own)
        trio = WC.at[0, 0, pl.ds(0, 3)]

        def start_row():
            for d in (1, 2, 3):
                copy(own, own, at_x(d), k).start()

        pl.when(source)(start_row)
        yield
        pl.when(jnp.logical_not(source))(row.wait_recv)
        col = send_group(trio, [(own, own, at_y(d)) for d in (2, 1, 3)])
        yield
        col.wait_recv()

        def block(d, lo=0, n=4):
            return WC.at[(z + d) % 8, c, pl.ds(lo, n)]

        b = block(0)
        up, down = send(b, b, at_z(1)), send(b, b, at_z(7))
        kt, tw = group(WC.at[:, 0])
        copy(b, b, twin, kt).start()
        yield
        for step in (1, 2, 3):
            n = 2 if step == 3 else 4
            up.wait_recv()
            b = block(8 - step, 0, n)
            up = send(b, b, at_z(1))
            down.wait_recv()
            b = block(step, 4 - n, n)
            down = send(b, b, at_z(7))
            for d in (8 - step, step):
                b = block(d)
                copy(b, b, twin, kt).start()
            yield
        up.wait_recv()
        down.wait_recv()
        b = block(4)
        copy(b, b, twin, kt).start()
        sent.append(tw)
        yield
        tw.wait_recv()
        pl.when(source)(copy(trio, trio, twin, k).wait_send)
        yield

    def scatter(h):
        if h == 0:
            me1, me2, ax1, ax2 = x, y, at_x, at_y
        else:
            me1, me2, ax1, ax2 = y, x, at_y, at_x

        def piece(buf, a, s, b):
            return buf.at[a % 4, s, b % 4, 0] if h == 0 else buf.at[b % 4, s, a % 4, 1]

        turn = (2, 1, 3, 0)
        far, near, both = {}, {}, {}

        def send_far(p):
            far[p] = [
                send_group(
                    R2.at[h, j, pl.ds(2 * p, 2)],
                    [(piece(Gs, me1 + 2, j, me2 + turn[q]), R2.at[h, j, q], to) for q in (2 * p, 2 * p + 1)],
                )
                for j, to in enumerate((ax1(1), ax1(3)))
            ]

        def send_near(p):
            near[p] = [
                send_group(
                    R1.at[h, j, 1 - j, pl.ds(2 * p, 2)],
                    [(piece(Gs, a, 1 - j, me2 + turn[q]), R1.at[h, j, 1 - j, q], to) for q in (2 * p, 2 * p + 1)],
                )
                for j, (a, to) in enumerate(((me1 + 1, ax1(1)), (me1 + 3, ax1(3))))
            ]

        def send_both(p):
            both[p] = []
            for j, (a, to) in enumerate(((me1 + 1, ax1(1)), (me1 + 3, ax1(3)))):
                far[p][j].wait_recv()
                copies = []
                for q in (2 * p, 2 * p + 1):
                    b = me2 + turn[q]
                    r = piece(Gs, a, j, b)
                    r[...] = (piece(G, a, j, b)[...] + R2[h, j, q].astype(F32)).astype(BF16)
                    copies.append((r, R1.at[h, j, j, q], to))
                both[p].append(send_group(R1.at[h, j, j, pl.ds(2 * p, 2)], copies))

        def arrived(p):
            for cp in (*near[p], *both[p]):
                cp.wait_recv()

        def total(q):
            b = me2 + turn[q]
            for s in range(2):
                g = piece(G, me1, s, b)
                v = g[...] + R1[h, 0, s, q].astype(F32) + R1[h, 1, s, q].astype(F32)
                g[...] = v
                piece(Gs, me1, s, b)[...] = v.astype(BF16)

        def two(buf, q, s):
            return piece(buf, me1, s, me2 + turn[q])

        send_far(0)
        yield
        send_far(1)
        yield
        send_near(0)
        yield
        send_both(0)
        yield
        send_near(1)
        yield
        send_both(1)
        yield
        arrived(0)
        total(0)
        far_p = send(two(Gs, 0, 0), Q2.at[h, 0], ax2(1))
        far_m = send(two(Gs, 0, 1), Q2.at[h, 1], ax2(3))
        total(1)
        near_p = send(two(Gs, 1, 1), Q1.at[h, 0, 1], ax2(1))
        yield
        far_p.wait_recv()
        two(Gs, 1, 0)[...] = (two(G, 1, 0)[...] + Q2[h, 0].astype(F32)).astype(BF16)
        both_p = send(two(Gs, 1, 0), Q1.at[h, 0, 0], ax2(1))
        yield
        arrived(1)
        total(2)
        near_m = send(two(Gs, 2, 0), Q1.at[h, 1, 0], ax2(3))
        far_m.wait_recv()
        two(Gs, 2, 1)[...] = (two(G, 2, 1)[...] + Q2[h, 1].astype(F32)).astype(BF16)
        both_m = send(two(Gs, 2, 1), Q1.at[h, 1, 1], ax2(3))
        total(3)
        yield
        for cp in (near_p, near_m, both_p, both_m):
            cp.wait_recv()
        away = 1 - zh
        two(Gs, 3, away)[...] = (
            two(G, 3, away)[...] + Q1[h, 0, away].astype(F32) + Q1[h, 1, away].astype(F32)
        ).astype(BF16)
        last = send(two(Gs, 3, away), Z3.at[h], at_z(4))
        yield
        mine = two(G, 3, zh)[...] + Q1[h, 0, zh].astype(F32) + Q1[h, 1, zh].astype(F32)
        last.wait_recv()
        res[pl.ds(16 * h, 16), :] = mine + Z3[h].astype(F32)
        yield

    def allreduce(k):
        cp = send(T.at[k, 1 - c], RC.at[k], twin)
        yield
        cp.wait_recv()
        A1[k] = T[k, c] + RC[k]
        got = send_group(
            RP.at[k],
            [
                (A1.at[k, (x + dx) % 4, (y + dy) % 4], RP.at[k, e], at_xy(dx, dy))
                for e, (dx, dy) in enumerate(plane)
            ],
        )
        yield
        got.wait_recv()
        v = A1[k, x, y]
        for e in range(len(plane)):
            v = v + RP[k, e]
        mine = RZ.at[k, z]
        mine[...] = v
        got = send_group(RZ.at[k, pl.ds(0, 7)], [(mine, mine, at_z(d)) for d in (4, 3, 5, 2, 6, 1, 7)])
        yield
        got.wait_recv()
        v = ((RZ[k, 0] + RZ[k, 1]) + (RZ[k, 2] + RZ[k, 3])) + ((RZ[k, 4] + RZ[k, 5]) + (RZ[k, 6] + RZ[k, 7]))
        mine = F.at[k, c * 4 + x, y]
        mine[...] = v
        got = send_group(RP.at[k], [(mine, mine, at_xy(*p)) for p in plane])
        yield
        got.wait_recv()
        half = F.at[k, pl.ds(c * 4, 4)]
        cp = send(half, half, twin)
        yield
        cp.wait_recv()
        yield

    def full(k):
        return jnp.concatenate([F[k, :, j].reshape(R, 512) for j in range(4)], axis=1)

    def put(k, v):
        for a in range(8):
            for j in range(4):
                T[k, a // 4, a % 4, j] = v[8 * a : 8 * (a + 1), 512 * j : 512 * (j + 1)]

    def my_rows(k):
        v = F[k, :, i // 16].reshape(R, 512)
        for n in (128, 32):
            place = (i // (n // 32)) % 4
            blk = v[:, :n]
            for j in range(1, 4):
                blk = jnp.where(place == j, v[:, n * j : n * (j + 1)], blk)
            v = blk
        return v

    own_w = [gather(True, h) for h in range(2)]
    oth_w = [gather(False, h) for h in range(2)]
    z_w = gather_z()
    grads = [scatter(h) for h in range(2)]
    red = [allreduce(k) for k in range(2)]

    def adv(*gens):
        for g in gens:
            next(g)

    def transpose_acts():
        for b in range(8):
            t = acts[:, 256 * b : 256 * (b + 1)].T
            for j in range(8):
                AT[j % 2, j // 2, pl.ds(32 * b, 32)] = t[32 * j : 32 * (j + 1)]

    def left_factor():
        basis_t = basis[...]
        b3 = split3(basis_t)
        u = fold3(nt(b3, go[...]))
        al.wait()
        p = fold3(nn(split3(u), acts[...]))
        el.wait()
        eb = jnp.concatenate([nt(basis_t, err[...], HI)] * 4, axis=1)
        col = lax.broadcasted_iota(jnp.int32, (R, D), 1)
        eb = jnp.where(col // 32 == i, jnp.concatenate([eb] * 16, axis=1), 0.0)
        put(0, (p * scale + eb) * (1.0 / GROUPS))

    def right_factor():
        pt = full(0)
        v = fold3(nt(split3(pt), acts[...]))
        s = fold3(nn(split3(v), go[...]))
        pe = nn(my_rows(0), err[...], HI)
        put(1, (s * scale + pe) * (1.0 / GROUPS))

    def gram():
        pt = full(0)
        row = lax.broadcasted_iota(jnp.int32, (R, R), 0)
        col = lax.broadcasted_iota(jnp.int32, (R, R), 1)
        M[...] = jnp.concatenate([nt(pt, pt, HI), (row == col).astype(F32)], axis=1)

    def factor(lo, hi):
        row = lax.broadcasted_iota(jnp.int32, (R, 2 * R), 0)
        col = lax.broadcasted_iota(jnp.int32, (R, 2 * R), 1)

        def body(k, m):
            rk = jnp.sum(jnp.where(row == k, m, 0.0), axis=0, keepdims=True)
            ck = jnp.sum(jnp.where(col == k, m, 0.0), axis=1, keepdims=True)
            piv = jnp.sum(jnp.where(col[:1] == k, rk, 0.0), axis=1, keepdims=True)
            rk = rk / jnp.sqrt(piv)
            ck = ck / jnp.sqrt(piv)
            return jnp.where(row > k, m - ck * rk, jnp.where(row == k, rk, m))

        M[...] = lax.fori_loop(lo, hi, body, M[...])

    def grad_own(d):
        a = (x + d) % 4

        def body(n, carry):
            cols = pl.ds(pl.multiple_of(n * 512, 512), 512)
            v = nn(AT[c, a], go[:, cols])
            G[a, :, :, :, :, cols] = v.reshape(2, 4, 2, 16, 512)
            return carry

        lax.fori_loop(0, 4, body, 0)

    def grad_twin(d):
        a = (x + d) % 4

        def body(n, carry):
            cols = pl.ds(pl.multiple_of(n * 512, 512), 512)
            v = nn(RT[a], go_tw[:, cols]).reshape(2, 4, 2, 16, 512)
            v = (v + G[a, :, :, :, :, cols]) * scale
            G[a, :, :, :, :, cols] = v
            Gs[a, :, :, :, :, cols] = v.astype(BF16)
            return carry

        lax.fori_loop(0, 4, body, 0)

    def grad_acts(*blocks):
        for j in blocks:
            s, b = j // 4, j % 4
            w = jnp.concatenate(
                [v for a in range(4) for k in range(2) for v in (WA[s, b, a, k], WC[s * 4 + (a + b) % 4, k, b])], axis=0
            )
            ga[:, 256 * j : 256 * (j + 1)] = nt(go[...], w).astype(BF16)

    def drain():
        while sent:
            sent.pop(0).wait_send()

    bl.wait()
    gl.wait()
    left_factor()
    wl[0].wait()
    pl.when(source)(wl[1].wait)
    pl.semaphore_wait(barrier, len(peers))
    adv(red[0])
    adv(*own_w)
    wz = send(WA.at[zh, y, x, c], WA.at[zh, y, x, c], mirror)
    adv(z_w)
    got = send(go, go_tw, twin)
    transpose_acts()
    att = send(AT.at[1 - c], RT, twin)
    grad_own(2)
    adv(red[0])
    grad_own(1)
    adv(*own_w)
    adv(z_w)
    grad_own(3)
    grad_own(0)
    adv(*own_w)
    wz.wait_recv()
    adv(*oth_w)
    adv(red[0])
    adv(z_w)
    got.wait_recv()
    att.wait_recv()
    grad_twin(2)
    adv(*own_w)
    grad_twin(1)
    adv(red[0])
    adv(grads[0])
    adv(grads[0])
    grad_twin(3)
    adv(grads[0])
    grad_twin(0)
    adv(grads[1])
    adv(grads[1])
    adv(grads[1])
    adv(*oth_w)
    adv(z_w)
    adv(red[0])
    adv(*own_w)
    adv(grads[0])
    adv(red[0])
    right_factor()
    adv(red[1])
    adv(grads[1])
    gram()
    adv(red[1])
    adv(*grads)
    factor(0, 16)
    adv(z_w)
    adv(*grads)
    factor(16, 32)
    adv(red[1])
    adv(*oth_w)
    adv(*grads)
    factor(32, 64)
    adv(red[1])
    ortho = nn(M[:, R:], my_rows(0), HI).T
    adv(z_w)
    adv(*grads)
    adv(*oth_w)
    adv(*own_w)
    adv(*grads)
    adv(z_w)
    adv(*oth_w)
    adv(red[1])
    adv(*grads)
    adv(z_w)
    adv(*oth_w)
    grad_acts(0, 1)
    adv(red[1])
    qf = nn(M[:, R:], full(1), HI)
    qt[...] = qf
    ap = nn(ortho, qf, HI)
    apv[...] = ap
    grad_acts(2, 3, 4, 5, 6, 7)
    adv(*grads)
    res[...] = res[...] + err[...] - ap
    drain()
    assert count[0] <= SEMS, count[0]
    for g in own_w + oth_w + [z_w] + grads + red:
        assert next(g, 0) == 0


def write_out(a, b, c, d, ao, bo, co, do, sem):
    cps = [pltpu.make_async_copy(v, o, sem.at[k]) for k, (v, o) in enumerate(((a, ao), (b, bo), (c, co), (d, do)))]
    for cp in cps:
        cp.start()
    for cp in cps:
        cp.wait()


def shards(acts, grad_out, weight, error, basis):
    scale = 1.0 / math.sqrt(TOK * lax.axis_size("inner"))
    hbm = pl.BlockSpec(memory_space=pltpu.HBM)
    vm = pltpu.VMEM
    ga, approx, err, qt = pl.pallas_call(
        functools.partial(kernel, scale),
        out_shape=(vm((TOK, D), BF16), vm((32, D), F32), vm((32, D), F32), vm((R, D), F32)),
        in_specs=[hbm] * 5,
        out_specs=(pl.BlockSpec(memory_space=vm),) * 4,
        scratch_shapes=[
            vm((TOK, D), BF16),
            vm((TOK, D), BF16),
            vm((32, D), F32),
            vm((R, D), F32),
            vm((2, 4, 4, 2, 16, D), BF16),
            vm((8, 2, 4, 16, D), BF16),
            vm((2, 4, 256, TOK), BF16),
            vm((4, 256, TOK), BF16),
            vm((TOK, D), BF16),
            vm((4, 2, 4, 2, 16, D), F32),
            vm((4, 2, 4, 2, 16, D), BF16),
            vm((2, 2, 2, 4, 16, D), BF16),
            vm((2, 2, 4, 16, D), BF16),
            vm((2, 2, 2, 16, D), BF16),
            vm((2, 2, 16, D), BF16),
            vm((2, 16, D), BF16),
            vm((2, 2, 4, 4, 8, 512), F32),
            vm((2, 4, 4, 8, 512), F32),
            vm((2, 4, 4, 8, 512), F32),
            vm((2, 15, 8, 512), F32),
            vm((2, 8, 8, 512), F32),
            vm((2, 8, 4, 8, 512), F32),
            vm((R, 2 * R), F32),
            pltpu.SemaphoreType.DMA((6,)),
            pltpu.SemaphoreType.DMA((SEMS,)),
            pltpu.SemaphoreType.DMA((SEMS,)),
        ],
        compiler_params=pltpu.CompilerParams(
            collective_id=0, has_side_effects=True, vmem_limit_bytes=60 * 2**20
        ),
        name="powersgd",
    )(acts, grad_out, weight, error[0], basis.T)
    ga, approx, err, qt = pl.pallas_call(
        write_out,
        out_shape=(
            jax.ShapeDtypeStruct((TOK, D), BF16),
            jax.ShapeDtypeStruct((32, D), F32),
            jax.ShapeDtypeStruct((32, D), F32),
            jax.ShapeDtypeStruct((R, D), F32),
        ),
        in_specs=[pl.BlockSpec(memory_space=pl.ANY)] * 4,
        out_specs=(hbm,) * 4,
        scratch_shapes=[pltpu.SemaphoreType.DMA((4,))],
        compiler_params=pltpu.CompilerParams(vmem_limit_bytes=2**20),
        name="write_out",
    )(ga, approx, err, qt)
    return (ga, approx, err[None], qt.T)


def solution(mesh):
    in_specs = (
        P(("inner", "outer"), None),
        P(("inner", "outer"), None),
        P("inner", None),
        P("outer", "inner", None),
        P(),
    )
    out_specs = (P(("inner", "outer"), None), P("inner", None), P("outer", "inner", None), P())
    return jax.shard_map(shards, mesh=mesh, in_specs=in_specs, out_specs=out_specs, check_vma=False)
```

```python
import functools
import math

import jax
import jax.numpy as jnp
from jax import lax
from jax.experimental import pallas as pl
from jax.experimental.pallas import tpu as pltpu
from jax.sharding import PartitionSpec as P

F32 = jnp.float32
BF16 = jnp.bfloat16
HI = lax.Precision.HIGHEST
MESH = pl.DeviceIdType.MESH

TOK = 512
D = 2048
R = 64
GROUPS = 4
SEMS = 94


def nn(a, b, precision=None):
    return lax.dot_general(a, b, (((1,), (0,)), ((), ())), precision=precision, preferred_element_type=F32)


def nt(a, b, precision=None):
    return lax.dot_general(a, b, (((1,), (1,)), ((), ())), precision=precision, preferred_element_type=F32)


def split3(v):
    hi = v.astype(BF16)
    rest = v - hi.astype(F32)
    mid = rest.astype(BF16)
    lo = (rest - mid.astype(F32)).astype(BF16)
    return jnp.concatenate([hi, mid, lo], axis=0)


def fold3(v):
    return v[:R] + (v[R : 2 * R] + v[2 * R :])


def kernel(
    scale,
    acts_hbm, go_hbm, weight_hbm, error_hbm, basis_hbm,
    ga, apv, res, qt,
    acts, go, err, basis, WA, WC, AT, RT, go_tw, G, Gs, R1, R2, Q1, Q2, Z3,
    T, RC, A1, RP, RP2, RZ, F, M,
    lsem, ssem, rsem,
):
    i = lax.axis_index("inner")
    zl = lax.axis_index("outer")
    zh, y, x, c = i // 32, (i // 8) % 4, (i // 2) % 4, i % 2
    z = zh * 4 + zl

    def dev(zh_, y_, x_, c_, zl_):
        return (((zh_ * 4 + y_) * 4 + x_) * 2 + c_, zl_)

    def at_x(d):
        return dev(zh, y, (x + d) % 4, c, zl)

    def at_y(d):
        return dev(zh, (y + d) % 4, x, c, zl)

    def at_xy(dx, dy):
        return dev(zh, (y + dy) % 4, (x + dx) % 4, c, zl)

    def at_z(d):
        zz = (z + d) % 8
        return dev(zz // 4, y, x, c, zz % 4)

    twin = dev(zh, y, x, 1 - c, zl)
    mirror = dev(1 - zh, y, x, c, 3 - zl)
    plane = sorted(
        [(dx, dy) for dx in range(4) for dy in range(4) if dx or dy],
        key=lambda p: -(min(p[0], 4 - p[0]) + min(p[1], 4 - p[1])),
    )

    count = [0]
    sent = []

    def copy(src, dst, to, k=None):
        if k is None:
            k = count[0]
            count[0] += 1
        return pltpu.make_async_remote_copy(
            src_ref=src, dst_ref=dst, send_sem=ssem.at[k], recv_sem=rsem.at[k], device_id=to, device_id_type=MESH
        )

    def send(src, dst, to):
        cp = copy(src, dst, to)
        cp.start()
        sent.append(cp)
        return cp

    def group(size):
        k = count[0]
        count[0] += 1
        return k, copy(size, size, twin, k)

    def send_group(size, copies):
        k, whole = group(size)
        for src, dst, to in copies:
            copy(src, dst, to, k).start()
        sent.append(whole)
        return whole

    source = (x + y) % 4 == zl
    wl = [
        pltpu.make_async_copy(weight_hbm.at[pl.ds(0, 16)], WA.at[zh, y, x, c], lsem.at[0]),
        pltpu.make_async_copy(weight_hbm.at[pl.ds(16, 16)], WC.at[z, c, y], lsem.at[1]),
    ]
    gl = pltpu.make_async_copy(go_hbm, go, lsem.at[2])
    al = pltpu.make_async_copy(acts_hbm, acts, lsem.at[3])
    bl = pltpu.make_async_copy(basis_hbm, basis, lsem.at[4])
    el = pltpu.make_async_copy(error_hbm, err, lsem.at[5])
    wl[0].start()
    pl.when(source)(wl[1].start)
    for cp in (bl, el, gl, al):
        cp.start()

    barrier = pltpu.get_barrier_semaphore()
    peers = [twin] + [at_xy(*p) for p in plane] + [at_z(d) for d in range(1, 8)]
    for p in peers:
        pl.semaphore_signal(barrier, inc=1, device_id=p, device_id_type=MESH)

    def gather(own, half):
        zs = zh if own else 1 - zh
        cols = pl.ds(half * (D // 2), D // 2)
        if half == 0:
            me1, me2, ax1, ax2 = x, y, at_x, at_y
        else:
            me1, me2, ax1, ax2 = y, x, at_y, at_x

        def piece(a):
            return WA.at[zs, y, a % 4, c, :, cols] if half == 0 else WA.at[zs, a % 4, x, c, :, cols]

        def block(b, lo=0, n=4):
            if half == 0:
                return WA.at[zs, b % 4, pl.ds(lo, n), c, :, cols]
            return WA.at[zs, pl.ds(lo, n), b % 4, c, :, cols]

        p = piece(me1)
        up = send(p, p, ax1(1))
        down = send(p, p, ax1(3))
        yield
        up.wait_recv()
        p = piece(me1 + 3)
        far = send(p, p, ax1(1))
        down.wait_recv()
        yield
        far.wait_recv()
        b = block(me2)
        up = send(b, b, ax2(1))
        down = send(b, b, ax2(3))
        k, tw = group(WA.at[0, :, :, 0, :, cols])
        copy(b, b, twin, k).start()
        yield
        up.wait_recv()
        b = block(me2 + 3, 0, 2)
        far_p = send(b, b, ax2(1))
        b = block(me2 + 3)
        copy(b, b, twin, k).start()
        down.wait_recv()
        b = block(me2 + 1, 2, 2)
        far_m = send(b, b, ax2(3))
        b = block(me2 + 1)
        copy(b, b, twin, k).start()
        yield
        far_p.wait_recv()
        far_m.wait_recv()
        b = block(me2 + 2)
        copy(b, b, twin, k).start()
        sent.append(tw)
        yield
        tw.wait_recv()
        yield

    def gather_z():
        own = WC.at[z, c, y]
        k, row = group(own)
        trio = WC.at[0, 0, pl.ds(0, 3)]

        def start_row():
            for d in (1, 2, 3):
                copy(own, own, at_x(d), k).start()

        pl.when(source)(start_row)
        yield
        pl.when(jnp.logical_not(source))(row.wait_recv)
        col = send_group(trio, [(own, own, at_y(d)) for d in (2, 1, 3)])
        yield
        col.wait_recv()

        def block(d, lo=0, n=4):
            return WC.at[(z + d) % 8, c, pl.ds(lo, n)]

        b = block(0)
        up, down = send(b, b, at_z(1)), send(b, b, at_z(7))
        kt, tw = group(WC.at[:, 0])
        copy(b, b, twin, kt).start()
        yield
        for step in (1, 2, 3):
            n = 2 if step == 3 else 4
            up.wait_recv()
            b = block(8 - step, 0, n)
            up = send(b, b, at_z(1))
            down.wait_recv()
            b = block(step, 4 - n, n)
            down = send(b, b, at_z(7))
            for d in (8 - step, step):
                b = block(d)
                copy(b, b, twin, kt).start()
            yield
        up.wait_recv()
        down.wait_recv()
        b = block(4)
        copy(b, b, twin, kt).start()
        sent.append(tw)
        yield
        tw.wait_recv()
        pl.when(source)(copy(trio, trio, twin, k).wait_send)
        yield

    def scatter(h):
        if h == 0:
            me1, me2, ax1, ax2 = x, y, at_x, at_y
        else:
            me1, me2, ax1, ax2 = y, x, at_y, at_x

        def piece(buf, a, s, b):
            return buf.at[a % 4, s, b % 4, 0] if h == 0 else buf.at[b % 4, s, a % 4, 1]

        turn = (2, 1, 3, 0)
        far, near, both = {}, {}, {}

        def send_far(p):
            far[p] = [
                send_group(
                    R2.at[h, j, pl.ds(2 * p, 2)],
                    [(piece(Gs, me1 + 2, j, me2 + turn[q]), R2.at[h, j, q], to) for q in (2 * p, 2 * p + 1)],
                )
                for j, to in enumerate((ax1(1), ax1(3)))
            ]

        def send_near(p):
            near[p] = [
                send_group(
                    R1.at[h, j, 1 - j, pl.ds(2 * p, 2)],
                    [(piece(Gs, a, 1 - j, me2 + turn[q]), R1.at[h, j, 1 - j, q], to) for q in (2 * p, 2 * p + 1)],
                )
                for j, (a, to) in enumerate(((me1 + 1, ax1(1)), (me1 + 3, ax1(3))))
            ]

        def send_both(p):
            both[p] = []
            for j, (a, to) in enumerate(((me1 + 1, ax1(1)), (me1 + 3, ax1(3)))):
                far[p][j].wait_recv()
                copies = []
                for q in (2 * p, 2 * p + 1):
                    b = me2 + turn[q]
                    r = piece(Gs, a, j, b)
                    r[...] = (piece(G, a, j, b)[...] + R2[h, j, q].astype(F32)).astype(BF16)
                    copies.append((r, R1.at[h, j, j, q], to))
                both[p].append(send_group(R1.at[h, j, j, pl.ds(2 * p, 2)], copies))

        def arrived(p):
            for cp in (*near[p], *both[p]):
                cp.wait_recv()

        def total(q):
            b = me2 + turn[q]
            for s in range(2):
                g = piece(G, me1, s, b)
                v = g[...] + R1[h, 0, s, q].astype(F32) + R1[h, 1, s, q].astype(F32)
                g[...] = v
                piece(Gs, me1, s, b)[...] = v.astype(BF16)

        def two(buf, q, s):
            return piece(buf, me1, s, me2 + turn[q])

        send_far(0)
        yield
        send_far(1)
        yield
        send_near(0)
        yield
        send_both(0)
        yield
        send_near(1)
        yield
        send_both(1)
        yield
        arrived(0)
        total(0)
        far_p = send(two(Gs, 0, 0), Q2.at[h, 0], ax2(1))
        far_m = send(two(Gs, 0, 1), Q2.at[h, 1], ax2(3))
        total(1)
        near_p = send(two(Gs, 1, 1), Q1.at[h, 0, 1], ax2(1))
        yield
        far_p.wait_recv()
        two(Gs, 1, 0)[...] = (two(G, 1, 0)[...] + Q2[h, 0].astype(F32)).astype(BF16)
        both_p = send(two(Gs, 1, 0), Q1.at[h, 0, 0], ax2(1))
        yield
        arrived(1)
        total(2)
        near_m = send(two(Gs, 2, 0), Q1.at[h, 1, 0], ax2(3))
        far_m.wait_recv()
        two(Gs, 2, 1)[...] = (two(G, 2, 1)[...] + Q2[h, 1].astype(F32)).astype(BF16)
        both_m = send(two(Gs, 2, 1), Q1.at[h, 1, 1], ax2(3))
        total(3)
        yield
        for cp in (near_p, near_m, both_p, both_m):
            cp.wait_recv()
        away = 1 - zh
        two(Gs, 3, away)[...] = (
            two(G, 3, away)[...] + Q1[h, 0, away].astype(F32) + Q1[h, 1, away].astype(F32)
        ).astype(BF16)
        last = send(two(Gs, 3, away), Z3.at[h], at_z(4))
        yield
        mine = two(G, 3, zh)[...] + Q1[h, 0, zh].astype(F32) + Q1[h, 1, zh].astype(F32)
        last.wait_recv()
        res[pl.ds(16 * h, 16), :] = mine + Z3[h].astype(F32)
        yield

    def allreduce(k):
        cp = send(T.at[k, 1 - c], RC.at[k], twin)
        yield
        cp.wait_recv()
        v = T[k, c] + RC[k]
        A1[k] = jnp.concatenate([v[..., :256], v[..., 256:]], axis=2).astype(BF16)
        got = send_group(
            RP.at[k],
            [
                (A1.at[k, (x + dx) % 4, (y + dy) % 4], RP.at[k, e], at_xy(dx, dy))
                for e, (dx, dy) in enumerate(plane)
            ],
        )
        yield
        got.wait_recv()
        v = RP[k, 0].astype(F32)
        for e in range(1, len(plane)):
            v = v + RP[k, e].astype(F32)
        v = T[k, c, x, y] + RC[k, x, y] + jnp.concatenate([v[:8], v[8:]], axis=1)
        mine = RZ.at[k, z]
        mine[...] = v
        got = send_group(RZ.at[k, pl.ds(0, 7)], [(mine, mine, at_z(d)) for d in (4, 3, 5, 2, 6, 1, 7)])
        yield
        got.wait_recv()
        v = ((RZ[k, 0] + RZ[k, 1]) + (RZ[k, 2] + RZ[k, 3])) + ((RZ[k, 4] + RZ[k, 5]) + (RZ[k, 6] + RZ[k, 7]))
        mine = F.at[k, c * 4 + x, y]
        mine[...] = v
        got = send_group(RP2, [(mine, mine, at_xy(*p)) for p in plane])
        yield
        got.wait_recv()
        half = F.at[k, pl.ds(c * 4, 4)]
        cp = send(half, half, twin)
        yield
        cp.wait_recv()
        yield

    def full(k):
        return jnp.concatenate([F[k, :, j].reshape(R, 512) for j in range(4)], axis=1)

    def put(k, v):
        for a in range(8):
            for j in range(4):
                T[k, a // 4, a % 4, j] = v[8 * a : 8 * (a + 1), 512 * j : 512 * (j + 1)]

    def my_rows(k):
        v = F[k, :, i // 16].reshape(R, 512)
        for n in (128, 32):
            place = (i // (n // 32)) % 4
            blk = v[:, :n]
            for j in range(1, 4):
                blk = jnp.where(place == j, v[:, n * j : n * (j + 1)], blk)
            v = blk
        return v

    own_w = [gather(True, h) for h in range(2)]
    oth_w = [gather(False, h) for h in range(2)]
    z_w = gather_z()
    grads = [scatter(h) for h in range(2)]
    red = [allreduce(k) for k in range(2)]

    def adv(*gens):
        for g in gens:
            next(g)

    def transpose_acts():
        for b in range(8):
            t = acts[:, 256 * b : 256 * (b + 1)].T
            for j in range(8):
                AT[j % 2, j // 2, pl.ds(32 * b, 32)] = t[32 * j : 32 * (j + 1)]

    def error_term():
        eb = jnp.concatenate([nt(basis[...], err[...], HI)] * 4, axis=1)
        col = lax.broadcasted_iota(jnp.int32, (R, D), 1)
        return jnp.where(col // 32 == i, jnp.concatenate([eb] * 16, axis=1), 0.0)

    def left_factor(eb):
        u = fold3(nt(split3(basis[...]), go[...]))
        al.wait()
        p = fold3(nn(split3(u), acts[...]))
        put(0, (p * scale + eb) * (1.0 / GROUPS))

    def right_factor():
        pt = full(0)
        v = fold3(nt(split3(pt), acts[...]))
        s = fold3(nn(split3(v), go[...]))
        pe = nn(my_rows(0), err[...], HI)
        put(1, (s * scale + pe) * (1.0 / GROUPS))

    def gram():
        pt = full(0)
        row = lax.broadcasted_iota(jnp.int32, (R, R), 0)
        col = lax.broadcasted_iota(jnp.int32, (R, R), 1)
        M[...] = jnp.concatenate([nt(pt, pt, HI), (row == col).astype(F32)], axis=1)

    def factor(lo, hi):
        row = lax.broadcasted_iota(jnp.int32, (R, 2 * R), 0)
        col = lax.broadcasted_iota(jnp.int32, (R, 2 * R), 1)

        def body(k, m):
            rk = jnp.sum(jnp.where(row == k, m, 0.0), axis=0, keepdims=True)
            ck = jnp.sum(jnp.where(col == k, m, 0.0), axis=1, keepdims=True)
            piv = jnp.sum(jnp.where(col[:1] == k, rk, 0.0), axis=1, keepdims=True)
            rk = rk / jnp.sqrt(piv)
            ck = ck / jnp.sqrt(piv)
            return jnp.where(row > k, m - ck * rk, jnp.where(row == k, rk, m))

        M[...] = lax.fori_loop(lo, hi, body, M[...])

    def grad_own(d):
        a = (x + d) % 4

        def body(n, carry):
            cols = pl.ds(pl.multiple_of(n * 512, 512), 512)
            v = nn(AT[c, a], go[:, cols])
            G[a, :, :, :, :, cols] = v.reshape(2, 4, 2, 16, 512)
            return carry

        lax.fori_loop(0, 4, body, 0)

    def grad_twin(d):
        a = (x + d) % 4

        def body(n, carry):
            cols = pl.ds(pl.multiple_of(n * 512, 512), 512)
            v = nn(RT[a], go_tw[:, cols]).reshape(2, 4, 2, 16, 512)
            v = (v + G[a, :, :, :, :, cols]) * scale
            G[a, :, :, :, :, cols] = v
            Gs[a, :, :, :, :, cols] = v.astype(BF16)
            return carry

        lax.fori_loop(0, 4, body, 0)

    def grad_acts(s, *blocks):
        for b in blocks:
            w = jnp.concatenate(
                [v for a in range(4) for k in range(2) for v in (WA[s, b, a, k], WC[s * 4 + (a + b) % 4, k, b])], axis=0
            )
            cols = pl.ds(pl.multiple_of((s * 4 + b) * 256, 256), 256)
            ga[:, cols] = nt(go[...], w).astype(BF16)

    def drain():
        while sent:
            sent.pop(0).wait_send()

    wl[0].wait()
    bl.wait()
    el.wait()
    eb = error_term()
    pl.when(source)(wl[1].wait)
    pl.semaphore_wait(barrier, len(peers))
    adv(*own_w)
    wz = send(WA.at[zh, y, x, c], WA.at[zh, y, x, c], mirror)
    adv(z_w)
    gl.wait()
    left_factor(eb)
    adv(red[0])
    got = [send(go, go_tw, twin)]
    transpose_acts()
    got.append(send(AT.at[1 - c], RT, twin))
    adv(red[0])
    adv(*own_w)
    adv(z_w)
    grad_own(2)
    grad_own(1)
    wz.wait_recv()
    adv(*oth_w)
    grad_own(3)
    grad_own(0)
    adv(red[0])
    adv(*own_w)
    adv(z_w)
    adv(*oth_w)
    for cp in got:
        cp.wait_recv()
    grad_twin(2)
    adv(*own_w)
    adv(red[0])
    adv(grads[0])
    adv(grads[0])
    grad_twin(1)
    grad_twin(3)
    adv(grads[0])
    grad_twin(0)
    adv(grads[1])
    adv(grads[1])
    adv(grads[1])
    adv(z_w)
    adv(red[0])
    adv(red[0])
    right_factor()
    adv(red[1])
    adv(grads[0])
    gram()
    adv(red[1])
    adv(grads[1])
    adv(*grads)
    factor(0, 16)
    adv(z_w)
    adv(*grads)
    adv(*oth_w)
    factor(16, 32)
    adv(red[1])
    adv(*grads)
    adv(*own_w)
    factor(32, 48)
    adv(*own_w)
    adv(z_w)
    factor(48, 64)
    adv(red[1])
    ortho = nn(M[:, R:], my_rows(0), HI).T
    adv(*grads)
    adv(z_w)
    adv(*grads)
    adv(z_w)
    grad_acts(zh, 0)
    adv(red[1])
    adv(*grads)
    adv(*oth_w)
    grad_acts(zh, 1)
    adv(red[1])
    qf = nn(M[:, R:], full(1), HI)
    qt[...] = qf
    ap = nn(ortho, qf, HI)
    apv[...] = ap
    adv(*oth_w)
    grad_acts(zh, 2, 3)
    adv(*oth_w)
    grad_acts(1 - zh, 0, 1, 2, 3)
    adv(*grads)
    res[...] = res[...] + err[...] - ap
    drain()
    assert count[0] <= SEMS, count[0]
    for g in own_w + oth_w + [z_w] + grads + red:
        assert next(g, 0) == 0


def write_out(a, b, c, d, ao, bo, co, do, sem):
    cps = [pltpu.make_async_copy(v, o, sem.at[k]) for k, (v, o) in enumerate(((a, ao), (b, bo), (c, co), (d, do)))]
    for cp in cps:
        cp.start()
    for cp in cps:
        cp.wait()


def shards(acts, grad_out, weight, error, basis):
    scale = 1.0 / math.sqrt(TOK * lax.axis_size("inner"))
    hbm = pl.BlockSpec(memory_space=pltpu.HBM)
    vm = pltpu.VMEM
    ga, approx, err, qt = pl.pallas_call(
        functools.partial(kernel, scale),
        out_shape=(vm((TOK, D), BF16), vm((32, D), F32), vm((32, D), F32), vm((R, D), F32)),
        in_specs=[hbm] * 5,
        out_specs=(pl.BlockSpec(memory_space=vm),) * 4,
        scratch_shapes=[
            vm((TOK, D), BF16),
            vm((TOK, D), BF16),
            vm((32, D), F32),
            vm((R, D), F32),
            vm((2, 4, 4, 2, 16, D), BF16),
            vm((8, 2, 4, 16, D), BF16),
            vm((2, 4, 256, TOK), BF16),
            vm((4, 256, TOK), BF16),
            vm((TOK, D), BF16),
            vm((4, 2, 4, 2, 16, D), F32),
            vm((4, 2, 4, 2, 16, D), BF16),
            vm((2, 2, 2, 4, 16, D), BF16),
            vm((2, 2, 4, 16, D), BF16),
            vm((2, 2, 2, 16, D), BF16),
            vm((2, 2, 16, D), BF16),
            vm((2, 16, D), BF16),
            vm((2, 2, 4, 4, 8, 512), F32),
            vm((2, 4, 4, 8, 512), F32),
            vm((2, 4, 4, 16, 256), BF16),
            vm((2, 15, 16, 256), BF16),
            vm((15, 8, 512), F32),
            vm((2, 8, 8, 512), F32),
            vm((2, 8, 4, 8, 512), F32),
            vm((R, 2 * R), F32),
            pltpu.SemaphoreType.DMA((6,)),
            pltpu.SemaphoreType.DMA((SEMS,)),
            pltpu.SemaphoreType.DMA((SEMS,)),
        ],
        compiler_params=pltpu.CompilerParams(
            collective_id=0, has_side_effects=True, vmem_limit_bytes=60 * 2**20
        ),
        name="powersgd",
    )(acts, grad_out, weight, error[0], basis.T)
    ga, approx, err, qt = pl.pallas_call(
        write_out,
        out_shape=(
            jax.ShapeDtypeStruct((TOK, D), BF16),
            jax.ShapeDtypeStruct((32, D), F32),
            jax.ShapeDtypeStruct((32, D), F32),
            jax.ShapeDtypeStruct((R, D), F32),
        ),
        in_specs=[pl.BlockSpec(memory_space=pl.ANY)] * 4,
        out_specs=(hbm,) * 4,
        scratch_shapes=[pltpu.SemaphoreType.DMA((4,))],
        compiler_params=pltpu.CompilerParams(vmem_limit_bytes=2**20),
        name="write_out",
    )(ga, approx, err, qt)
    return (ga, approx, err[None], qt.T)


def solution(mesh):
    in_specs = (
        P(("inner", "outer"), None),
        P(("inner", "outer"), None),
        P("inner", None),
        P("outer", "inner", None),
        P(),
    )
    out_specs = (P(("inner", "outer"), None), P("inner", None), P("outer", "inner", None), P())
    return jax.shard_map(shards, mesh=mesh, in_specs=in_specs, out_specs=out_specs, check_vma=False)
```

```python
import functools
import math

import jax
import jax.numpy as jnp
from jax import lax
from jax.experimental import pallas as pl
from jax.experimental.pallas import tpu as pltpu
from jax.sharding import PartitionSpec as P

F32 = jnp.float32
BF16 = jnp.bfloat16
HI = lax.Precision.HIGHEST
MESH = pl.DeviceIdType.MESH

TOK = 512
D = 2048
R = 64
GROUPS = 4
RECV = 94
SEND = 27


def nn(a, b, precision=None):
    return lax.dot_general(a, b, (((1,), (0,)), ((), ())), precision=precision, preferred_element_type=F32)


def nt(a, b, precision=None):
    return lax.dot_general(a, b, (((1,), (1,)), ((), ())), precision=precision, preferred_element_type=F32)


def split3(v):
    hi = v.astype(BF16)
    rest = v - hi.astype(F32)
    mid = rest.astype(BF16)
    lo = (rest - mid.astype(F32)).astype(BF16)
    return jnp.concatenate([hi, mid, lo], axis=0)


def fold3(v):
    return v[:R] + (v[R : 2 * R] + v[2 * R :])


def kernel(
    scale,
    acts_hbm, go_hbm, weight_hbm, error_hbm, basis_hbm,
    ga, apv, res, qt,
    acts, go, err, basis, WA, WC, AT, RT, go_tw, G, Gs, R1, R2, Q1, Q2, Z3,
    T, RC, A1, RP, RP2, RZ, F, M,
    lsem, ssem, rsem,
):
    i = lax.axis_index("inner")
    zl = lax.axis_index("outer")
    zh, y, x, c = i // 32, (i // 8) % 4, (i // 2) % 4, i % 2
    z = zh * 4 + zl

    def dev(zh_, y_, x_, c_, zl_):
        return (((zh_ * 4 + y_) * 4 + x_) * 2 + c_, zl_)

    def at_x(d):
        return dev(zh, y, (x + d) % 4, c, zl)

    def at_y(d):
        return dev(zh, (y + d) % 4, x, c, zl)

    def at_xy(dx, dy):
        return dev(zh, (y + dy) % 4, (x + dx) % 4, c, zl)

    def at_z(d):
        zz = (z + d) % 8
        return dev(zz // 4, y, x, c, zz % 4)

    twin = dev(zh, y, x, 1 - c, zl)
    mirror = dev(1 - zh, y, x, c, 3 - zl)
    plane = sorted(
        [(dx, dy) for dx in range(4) for dy in range(4) if dx or dy],
        key=lambda p: -(min(p[0], 4 - p[0]) + min(p[1], 4 - p[1])),
    )

    count = [0, 0]
    sent = []

    def take(j):
        count[j] += 1
        return count[j] - 1

    def copy(src, dst, to, k, ks):
        return pltpu.make_async_remote_copy(
            src_ref=src, dst_ref=dst, send_sem=ssem.at[ks], recv_sem=rsem.at[k], device_id=to, device_id_type=MESH
        )

    def together(size):
        ks = take(1)
        sent.append(copy(size, size, twin, 0, ks))
        return ks

    def send(src, dst, to, ks=None):
        cp = copy(src, dst, to, take(0), together(src) if ks is None else ks)
        cp.start()
        return cp

    def group(size, ks=None):
        k, ks = take(0), together(size) if ks is None else ks
        return copy(size, size, twin, k, ks), lambda src, dst, to: copy(src, dst, to, k, ks).start()

    def send_group(size, copies, ks=None):
        whole, start = group(size, ks)
        for c3 in copies:
            start(*c3)
        return whole

    source = (x + y) % 4 == zl
    wl = [
        pltpu.make_async_copy(weight_hbm.at[pl.ds(0, 16)], WA.at[zh, y, x, c], lsem.at[0]),
        pltpu.make_async_copy(weight_hbm.at[pl.ds(16, 16)], WC.at[z, c, y], lsem.at[1]),
    ]
    gl = pltpu.make_async_copy(go_hbm, go, lsem.at[2])
    al = pltpu.make_async_copy(acts_hbm, acts, lsem.at[3])
    bl = pltpu.make_async_copy(basis_hbm, basis, lsem.at[4])
    el = pltpu.make_async_copy(error_hbm, err, lsem.at[5])
    wl[0].start()
    pl.when(source)(wl[1].start)
    for cp in (bl, el, gl, al):
        cp.start()

    barrier = pltpu.get_barrier_semaphore()
    peers = [twin] + [at_xy(*p) for p in plane] + [at_z(d) for d in range(1, 8)]
    for p in peers:
        pl.semaphore_signal(barrier, inc=1, device_id=p, device_id_type=MESH)

    def gather(own, half):
        zs = zh if own else 1 - zh
        cols = pl.ds(half * (D // 2), D // 2)
        if half == 0:
            me1, me2, ax1, ax2 = x, y, at_x, at_y
        else:
            me1, me2, ax1, ax2 = y, x, at_y, at_x

        def piece(a):
            return WA.at[zs, y, a % 4, c, :, cols] if half == 0 else WA.at[zs, a % 4, x, c, :, cols]

        def block(b, lo=0, n=4):
            if half == 0:
                return WA.at[zs, b % 4, pl.ds(lo, n), c, :, cols]
            return WA.at[zs, pl.ds(lo, n), b % 4, c, :, cols]

        ks = together(WA.at[0, 0, pl.ds(0, 3), 0, :, cols])
        p = piece(me1)
        up = send(p, p, ax1(1), ks)
        down = send(p, p, ax1(3), ks)
        yield
        up.wait_recv()
        p = piece(me1 + 3)
        far = send(p, p, ax1(1), ks)
        down.wait_recv()
        yield
        far.wait_recv()
        ks = together(go_tw.at[pl.ds(0, 224)])
        b = block(me2)
        up = send(b, b, ax2(1), ks)
        down = send(b, b, ax2(3), ks)
        tw, to_twin = group(WA.at[0, :, :, 0, :, cols], ks)
        to_twin(b, b, twin)
        yield
        up.wait_recv()
        b = block(me2 + 3, 0, 2)
        far_p = send(b, b, ax2(1), ks)
        b = block(me2 + 3)
        to_twin(b, b, twin)
        down.wait_recv()
        b = block(me2 + 1, 2, 2)
        far_m = send(b, b, ax2(3), ks)
        b = block(me2 + 1)
        to_twin(b, b, twin)
        yield
        far_p.wait_recv()
        far_m.wait_recv()
        b = block(me2 + 2)
        to_twin(b, b, twin)
        yield
        tw.wait_recv()
        yield

    def gather_z():
        own = WC.at[z, c, y]
        row_ks = take(1)
        row, to_row = group(own, row_ks)
        trio = WC.at[0, 0, pl.ds(0, 3)]

        def start_row():
            for d in (1, 2, 3):
                to_row(own, own, at_x(d))

        pl.when(source)(start_row)
        yield
        pl.when(jnp.logical_not(source))(row.wait_recv)
        col = send_group(trio, [(own, own, at_y(d)) for d in (2, 1, 3)])
        yield
        col.wait_recv()

        def block(d, lo=0, n=4):
            return WC.at[(z + d) % 8, c, pl.ds(lo, n)]

        b = block(0)
        ks = together(go_tw.at[pl.ds(0, 448)])
        up, down = send(b, b, at_z(1), ks), send(b, b, at_z(7), ks)
        tw, to_twin = group(WC.at[:, 0])
        to_twin(b, b, twin)
        yield
        for step in (1, 2, 3):
            n = 2 if step == 3 else 4
            up.wait_recv()
            b = block(8 - step, 0, n)
            up = send(b, b, at_z(1), ks)
            down.wait_recv()
            b = block(step, 4 - n, n)
            down = send(b, b, at_z(7), ks)
            for d in (8 - step, step):
                b = block(d)
                to_twin(b, b, twin)
            yield
        up.wait_recv()
        down.wait_recv()
        b = block(4)
        to_twin(b, b, twin)
        yield
        tw.wait_recv()
        pl.when(source)(copy(trio, trio, twin, 0, row_ks).wait_send)
        yield

    def scatter(h):
        if h == 0:
            me1, me2, ax1, ax2 = x, y, at_x, at_y
        else:
            me1, me2, ax1, ax2 = y, x, at_y, at_x

        def piece(buf, a, s, b):
            return buf.at[a % 4, s, b % 4, 0] if h == 0 else buf.at[b % 4, s, a % 4, 1]

        ks = together(go_tw.at[pl.ds(0, 496)])
        turn = (2, 1, 3, 0)
        far, near, both = {}, {}, {}

        def send_far(p):
            far[p] = [
                send_group(
                    R2.at[h, j, pl.ds(2 * p, 2)],
                    [(piece(Gs, me1 + 2, j, me2 + turn[q]), R2.at[h, j, q], to) for q in (2 * p, 2 * p + 1)],
                    ks,
                )
                for j, to in enumerate((ax1(1), ax1(3)))
            ]

        def send_near(p):
            near[p] = [
                send_group(
                    R1.at[h, j, 1 - j, pl.ds(2 * p, 2)],
                    [(piece(Gs, a, 1 - j, me2 + turn[q]), R1.at[h, j, 1 - j, q], to) for q in (2 * p, 2 * p + 1)],
                    ks,
                )
                for j, (a, to) in enumerate(((me1 + 1, ax1(1)), (me1 + 3, ax1(3))))
            ]

        def send_both(p):
            both[p] = []
            for j, (a, to) in enumerate(((me1 + 1, ax1(1)), (me1 + 3, ax1(3)))):
                far[p][j].wait_recv()
                copies = []
                for q in (2 * p, 2 * p + 1):
                    b = me2 + turn[q]
                    r = piece(Gs, a, j, b)
                    r[...] = (piece(G, a, j, b)[...] + R2[h, j, q].astype(F32)).astype(BF16)
                    copies.append((r, R1.at[h, j, j, q], to))
                both[p].append(send_group(R1.at[h, j, j, pl.ds(2 * p, 2)], copies, ks))

        def arrived(p):
            for cp in (*near[p], *both[p]):
                cp.wait_recv()

        def total(q):
            b = me2 + turn[q]
            for s in range(2):
                g = piece(G, me1, s, b)
                v = g[...] + R1[h, 0, s, q].astype(F32) + R1[h, 1, s, q].astype(F32)
                g[...] = v
                piece(Gs, me1, s, b)[...] = v.astype(BF16)

        def two(buf, q, s):
            return piece(buf, me1, s, me2 + turn[q])

        send_far(0)
        yield
        send_far(1)
        yield
        send_near(0)
        yield
        send_both(0)
        yield
        send_near(1)
        yield
        send_both(1)
        yield
        arrived(0)
        total(0)
        far_p = send(two(Gs, 0, 0), Q2.at[h, 0], ax2(1), ks)
        far_m = send(two(Gs, 0, 1), Q2.at[h, 1], ax2(3), ks)
        total(1)
        near_p = send(two(Gs, 1, 1), Q1.at[h, 0, 1], ax2(1), ks)
        yield
        far_p.wait_recv()
        two(Gs, 1, 0)[...] = (two(G, 1, 0)[...] + Q2[h, 0].astype(F32)).astype(BF16)
        both_p = send(two(Gs, 1, 0), Q1.at[h, 0, 0], ax2(1), ks)
        yield
        arrived(1)
        total(2)
        near_m = send(two(Gs, 2, 0), Q1.at[h, 1, 0], ax2(3), ks)
        far_m.wait_recv()
        two(Gs, 2, 1)[...] = (two(G, 2, 1)[...] + Q2[h, 1].astype(F32)).astype(BF16)
        both_m = send(two(Gs, 2, 1), Q1.at[h, 1, 1], ax2(3), ks)
        total(3)
        yield
        for cp in (near_p, near_m, both_p, both_m):
            cp.wait_recv()
        away = 1 - zh
        two(Gs, 3, away)[...] = (
            two(G, 3, away)[...] + Q1[h, 0, away].astype(F32) + Q1[h, 1, away].astype(F32)
        ).astype(BF16)
        last = send(two(Gs, 3, away), Z3.at[h], at_z(4), ks)
        yield
        mine = two(G, 3, zh)[...] + Q1[h, 0, zh].astype(F32) + Q1[h, 1, zh].astype(F32)
        last.wait_recv()
        res[pl.ds(16 * h, 16), :] = mine + Z3[h].astype(F32)
        yield

    def allreduce(k):
        cp = send(T.at[k, 1 - c], RC.at[k], twin)
        yield
        cp.wait_recv()
        v = T[k, c] + RC[k]
        A1[k] = jnp.concatenate([v[..., :256], v[..., 256:]], axis=2).astype(BF16)
        got = send_group(
            RP.at[k],
            [
                (A1.at[k, (x + dx) % 4, (y + dy) % 4], RP.at[k, e], at_xy(dx, dy))
                for e, (dx, dy) in enumerate(plane)
            ],
        )
        yield
        got.wait_recv()
        v = RP[k, 0].astype(F32)
        for e in range(1, len(plane)):
            v = v + RP[k, e].astype(F32)
        v = T[k, c, x, y] + RC[k, x, y] + jnp.concatenate([v[:8], v[8:]], axis=1)
        mine = RZ.at[k, z]
        mine[...] = v
        got = send_group(RZ.at[k, pl.ds(0, 7)], [(mine, mine, at_z(d)) for d in (4, 3, 5, 2, 6, 1, 7)])
        yield
        got.wait_recv()
        v = ((RZ[k, 0] + RZ[k, 1]) + (RZ[k, 2] + RZ[k, 3])) + ((RZ[k, 4] + RZ[k, 5]) + (RZ[k, 6] + RZ[k, 7]))
        mine = F.at[k, c * 4 + x, y]
        mine[...] = v
        got = send_group(RP2, [(mine, mine, at_xy(*p)) for p in plane])
        yield
        got.wait_recv()
        half = F.at[k, pl.ds(c * 4, 4)]
        cp = send(half, half, twin)
        yield
        cp.wait_recv()
        yield

    def full(k):
        return jnp.concatenate([F[k, :, j].reshape(R, 512) for j in range(4)], axis=1)

    def put(k, v):
        for a in range(8):
            for j in range(4):
                T[k, a // 4, a % 4, j] = v[8 * a : 8 * (a + 1), 512 * j : 512 * (j + 1)]

    def my_rows(k):
        v = F[k, :, i // 16].reshape(R, 512)
        for n in (128, 32):
            place = (i // (n // 32)) % 4
            blk = v[:, :n]
            for j in range(1, 4):
                blk = jnp.where(place == j, v[:, n * j : n * (j + 1)], blk)
            v = blk
        return v

    own_w = [gather(True, h) for h in range(2)]
    oth_w = [gather(False, h) for h in range(2)]
    z_w = gather_z()
    grads = [scatter(h) for h in range(2)]
    red = [allreduce(k) for k in range(2)]

    def adv(*gens):
        for g in gens:
            next(g)

    def transpose_acts():
        for b in range(8):
            t = acts[:, 256 * b : 256 * (b + 1)].T
            for j in range(8):
                AT[j % 2, j // 2, pl.ds(32 * b, 32)] = t[32 * j : 32 * (j + 1)]

    def error_term(b3):
        eb = fold3(nt(b3, split3(err[...])))
        eb = jnp.concatenate([eb[:, :32] + (eb[:, 32:64] + eb[:, 64:])] * 4, axis=1)
        col = lax.broadcasted_iota(jnp.int32, (R, D), 1)
        return jnp.where(col // 32 == i, jnp.concatenate([eb] * 16, axis=1), 0.0)

    def left_factor(b3, eb):
        u = fold3(nt(b3, go[...]))
        al.wait()
        p = fold3(nn(split3(u), acts[...]))
        put(0, (p * scale + eb) * (1.0 / GROUPS))

    def right_factor():
        pt = full(0)
        v = fold3(nt(split3(pt), acts[...]))
        s = fold3(nn(split3(v), go[...]))
        pe = nn(my_rows(0), err[...], HI)
        put(1, (s * scale + pe) * (1.0 / GROUPS))

    def gram():
        pt = full(0)
        row = lax.broadcasted_iota(jnp.int32, (R, R), 0)
        col = lax.broadcasted_iota(jnp.int32, (R, R), 1)
        M[...] = jnp.concatenate([nt(pt, pt, HI), (row == col).astype(F32)], axis=1)

    def factor(lo, hi):
        row = lax.broadcasted_iota(jnp.int32, (R, 2 * R), 0)
        col = lax.broadcasted_iota(jnp.int32, (R, 2 * R), 1)

        def body(k, m):
            rk = jnp.sum(jnp.where(row == k, m, 0.0), axis=0, keepdims=True)
            ck = jnp.sum(jnp.where(col == k, m, 0.0), axis=1, keepdims=True)
            piv = jnp.sum(jnp.where(col[:1] == k, rk, 0.0), axis=1, keepdims=True)
            rk = rk / jnp.sqrt(piv)
            ck = ck / jnp.sqrt(piv)
            return jnp.where(row > k, m - ck * rk, jnp.where(row == k, rk, m))

        M[...] = lax.fori_loop(lo, hi, body, M[...])

    def grad_own(d):
        a = (x + d) % 4

        def body(n, carry):
            cols = pl.ds(pl.multiple_of(n * 512, 512), 512)
            v = nn(AT[c, a], go[:, cols])
            G[a, :, :, :, :, cols] = v.reshape(2, 4, 2, 16, 512)
            return carry

        lax.fori_loop(0, 4, body, 0)

    def grad_twin(d):
        a = (x + d) % 4

        def body(n, carry):
            cols = pl.ds(pl.multiple_of(n * 512, 512), 512)
            v = nn(RT[a], go_tw[:, cols]).reshape(2, 4, 2, 16, 512)
            v = (v + G[a, :, :, :, :, cols]) * scale
            G[a, :, :, :, :, cols] = v
            Gs[a, :, :, :, :, cols] = v.astype(BF16)
            return carry

        lax.fori_loop(0, 4, body, 0)

    def grad_acts(s, *blocks):
        for b in blocks:
            w = jnp.concatenate(
                [v for a in range(4) for k in range(2) for v in (WA[s, b, a, k], WC[s * 4 + (a + b) % 4, k, b])], axis=0
            )
            cols = pl.ds(pl.multiple_of((s * 4 + b) * 256, 256), 256)
            ga[:, cols] = nt(go[...], w).astype(BF16)

    def drain():
        while sent:
            sent.pop(0).wait_send()

    wl[0].wait()
    bl.wait()
    b3 = split3(basis[...])
    el.wait()
    eb = error_term(b3)
    pl.when(source)(wl[1].wait)
    pl.semaphore_wait(barrier, len(peers))
    adv(*own_w)
    wz = send(WA.at[zh, y, x, c], WA.at[zh, y, x, c], mirror)
    adv(z_w)
    gl.wait()
    left_factor(b3, eb)
    adv(red[0])
    got = [send(go, go_tw, twin)]
    transpose_acts()
    got.append(send(AT.at[1 - c], RT, twin))
    adv(red[0])
    adv(*own_w)
    adv(z_w)
    grad_own(2)
    grad_own(1)
    adv(red[0])
    wz.wait_recv()
    adv(*oth_w)
    grad_own(3)
    adv(*own_w)
    adv(z_w)
    grad_own(0)
    adv(*oth_w)
    for cp in got:
        cp.wait_recv()
    grad_twin(2)
    adv(red[0])
    adv(*own_w)
    adv(grads[0])
    adv(grads[0])
    grad_twin(1)
    grad_twin(3)
    adv(grads[0])
    grad_twin(0)
    adv(grads[1])
    adv(grads[1])
    adv(grads[1])
    adv(red[0])
    adv(z_w)
    adv(red[0])
    right_factor()
    adv(red[1])
    gram()
    adv(red[1])
    adv(*grads)
    adv(*grads)
    factor(0, 16)
    adv(z_w)
    adv(*grads)
    factor(16, 32)
    adv(red[1])
    adv(*grads)
    adv(*oth_w)
    adv(*own_w)
    factor(32, 48)
    adv(*own_w)
    adv(z_w)
    factor(48, 64)
    adv(red[1])
    ortho = nn(M[:, R:], my_rows(0), HI).T
    adv(*grads)
    adv(*grads)
    adv(z_w)
    adv(z_w)
    grad_acts(zh, 0, 1)
    adv(red[1])
    adv(*oth_w)
    adv(*grads)
    adv(red[1])
    qf = nn(M[:, R:], full(1), HI)
    qt[...] = qf
    ap = nn(ortho, qf, HI)
    apv[...] = ap
    adv(*oth_w)
    grad_acts(zh, 2, 3)
    adv(*oth_w)
    grad_acts(1 - zh, 0, 1, 2, 3)
    adv(*grads)
    res[...] = res[...] + err[...] - ap
    drain()
    assert count[0] == RECV and count[1] == SEND, count
    for g in own_w + oth_w + [z_w] + grads + red:
        assert next(g, 0) == 0


def write_out(a, b, c, d, ao, bo, co, do, sem):
    cps = [pltpu.make_async_copy(v, o, sem.at[k]) for k, (v, o) in enumerate(((a, ao), (b, bo), (c, co), (d, do)))]
    for cp in cps:
        cp.start()
    for cp in cps:
        cp.wait()


def shards(acts, grad_out, weight, error, basis):
    scale = 1.0 / math.sqrt(TOK * lax.axis_size("inner"))
    hbm = pl.BlockSpec(memory_space=pltpu.HBM)
    vm = pltpu.VMEM
    ga, approx, err, qt = pl.pallas_call(
        functools.partial(kernel, scale),
        out_shape=(vm((TOK, D), BF16), vm((32, D), F32), vm((32, D), F32), vm((R, D), F32)),
        in_specs=[hbm] * 5,
        out_specs=(pl.BlockSpec(memory_space=vm),) * 4,
        scratch_shapes=[
            vm((TOK, D), BF16),
            vm((TOK, D), BF16),
            vm((32, D), F32),
            vm((R, D), F32),
            vm((2, 4, 4, 2, 16, D), BF16),
            vm((8, 2, 4, 16, D), BF16),
            vm((2, 4, 256, TOK), BF16),
            vm((4, 256, TOK), BF16),
            vm((TOK, D), BF16),
            vm((4, 2, 4, 2, 16, D), F32),
            vm((4, 2, 4, 2, 16, D), BF16),
            vm((2, 2, 2, 4, 16, D), BF16),
            vm((2, 2, 4, 16, D), BF16),
            vm((2, 2, 2, 16, D), BF16),
            vm((2, 2, 16, D), BF16),
            vm((2, 16, D), BF16),
            vm((2, 2, 4, 4, 8, 512), F32),
            vm((2, 4, 4, 8, 512), F32),
            vm((2, 4, 4, 16, 256), BF16),
            vm((2, 15, 16, 256), BF16),
            vm((15, 8, 512), F32),
            vm((2, 8, 8, 512), F32),
            vm((2, 8, 4, 8, 512), F32),
            vm((R, 2 * R), F32),
            pltpu.SemaphoreType.DMA((6,)),
            pltpu.SemaphoreType.DMA((SEND,)),
            pltpu.SemaphoreType.DMA((RECV,)),
        ],
        compiler_params=pltpu.CompilerParams(
            collective_id=0, has_side_effects=True, vmem_limit_bytes=60 * 2**20
        ),
        name="powersgd",
    )(acts, grad_out, weight, error[0], basis.T)
    ga, approx, err, qt = pl.pallas_call(
        write_out,
        out_shape=(
            jax.ShapeDtypeStruct((TOK, D), BF16),
            jax.ShapeDtypeStruct((32, D), F32),
            jax.ShapeDtypeStruct((32, D), F32),
            jax.ShapeDtypeStruct((R, D), F32),
        ),
        in_specs=[pl.BlockSpec(memory_space=pl.ANY)] * 4,
        out_specs=(hbm,) * 4,
        scratch_shapes=[pltpu.SemaphoreType.DMA((4,))],
        compiler_params=pltpu.CompilerParams(vmem_limit_bytes=2**20),
        name="write_out",
    )(ga, approx, err, qt)
    return (ga, approx, err[None], qt.T)


def solution(mesh):
    in_specs = (
        P(("inner", "outer"), None),
        P(("inner", "outer"), None),
        P("inner", None),
        P("outer", "inner", None),
        P(),
    )
    out_specs = (P(("inner", "outer"), None), P("inner", None), P("outer", "inner", None), P())
    return jax.shard_map(shards, mesh=mesh, in_specs=in_specs, out_specs=out_specs, check_vma=False)
```

```python
import functools
import math

import jax
import jax.numpy as jnp
from jax import lax
from jax.experimental import pallas as pl
from jax.experimental.pallas import tpu as pltpu
from jax.sharding import PartitionSpec as P

F32 = jnp.float32
BF16 = jnp.bfloat16
HI = lax.Precision.HIGHEST
MESH = pl.DeviceIdType.MESH

TOK = 512
D = 2048
R = 64
GROUPS = 4
RECV = 94
SEND = 27


def nn(a, b, precision=None):
    return lax.dot_general(a, b, (((1,), (0,)), ((), ())), precision=precision, preferred_element_type=F32)


def nt(a, b, precision=None):
    return lax.dot_general(a, b, (((1,), (1,)), ((), ())), precision=precision, preferred_element_type=F32)


def split3(v):
    hi = v.astype(BF16)
    rest = v - hi.astype(F32)
    mid = rest.astype(BF16)
    lo = (rest - mid.astype(F32)).astype(BF16)
    return jnp.concatenate([hi, mid, lo], axis=0)


def fold3(v):
    return v[:R] + (v[R : 2 * R] + v[2 * R :])


def kernel(
    scale,
    acts_hbm, go_hbm, weight_hbm, error_hbm, basis_hbm,
    ga, apv, res, qt,
    acts, go, err, basis, WA, WC, AT, RT, go_tw, G, Gs, R1, R2, Q1, Q2, Z3,
    T, RC, A1, RP, RP2, RZ, F, M,
    lsem, ssem, rsem,
):
    i = lax.axis_index("inner")
    zl = lax.axis_index("outer")
    zh, y, x, c = i // 32, (i // 8) % 4, (i // 2) % 4, i % 2
    z = zh * 4 + zl

    def dev(zh_, y_, x_, c_, zl_):
        return (((zh_ * 4 + y_) * 4 + x_) * 2 + c_, zl_)

    def at_x(d):
        return dev(zh, y, (x + d) % 4, c, zl)

    def at_y(d):
        return dev(zh, (y + d) % 4, x, c, zl)

    def at_xy(dx, dy):
        return dev(zh, (y + dy) % 4, (x + dx) % 4, c, zl)

    def at_z(d):
        zz = (z + d) % 8
        return dev(zz // 4, y, x, c, zz % 4)

    twin = dev(zh, y, x, 1 - c, zl)
    mirror = dev(1 - zh, y, x, c, 3 - zl)
    plane = sorted(
        [(dx, dy) for dx in range(4) for dy in range(4) if dx or dy],
        key=lambda p: -(min(p[0], 4 - p[0]) + min(p[1], 4 - p[1])),
    )

    count = [0, 0]
    sent = []

    def take(j):
        count[j] += 1
        return count[j] - 1

    def copy(src, dst, to, k, ks):
        return pltpu.make_async_remote_copy(
            src_ref=src, dst_ref=dst, send_sem=ssem.at[ks], recv_sem=rsem.at[k], device_id=to, device_id_type=MESH
        )

    def together(size):
        ks = take(1)
        sent.append(copy(size, size, twin, 0, ks))
        return ks

    def send(src, dst, to, ks=None):
        cp = copy(src, dst, to, take(0), together(src) if ks is None else ks)
        cp.start()
        return cp

    def group(size, ks=None):
        k, ks = take(0), together(size) if ks is None else ks
        return copy(size, size, twin, k, ks), lambda src, dst, to: copy(src, dst, to, k, ks).start()

    def send_group(size, copies, ks=None):
        whole, start = group(size, ks)
        for c3 in copies:
            start(*c3)
        return whole

    source = (x + y) % 4 == zl
    wl = [
        pltpu.make_async_copy(weight_hbm.at[pl.ds(0, 16)], WA.at[zh, y, x, c], lsem.at[0]),
        pltpu.make_async_copy(weight_hbm.at[pl.ds(16, 16)], WC.at[z, c, y], lsem.at[1]),
    ]
    gl = pltpu.make_async_copy(go_hbm, go, lsem.at[2])
    al = pltpu.make_async_copy(acts_hbm, acts, lsem.at[3])
    bl = pltpu.make_async_copy(basis_hbm, basis, lsem.at[4])
    el = pltpu.make_async_copy(error_hbm, err, lsem.at[5])
    wl[0].start()
    pl.when(source)(wl[1].start)
    for cp in (bl, el, gl, al):
        cp.start()

    barrier = pltpu.get_barrier_semaphore()
    peers = [twin] + [at_xy(*p) for p in plane] + [at_z(d) for d in range(1, 8)]
    for p in peers:
        pl.semaphore_signal(barrier, inc=1, device_id=p, device_id_type=MESH)

    def gather(own, half):
        zs = zh if own else 1 - zh
        cols = pl.ds(half * (D // 2), D // 2)
        if half == 0:
            me1, me2, ax1, ax2 = x, y, at_x, at_y
        else:
            me1, me2, ax1, ax2 = y, x, at_y, at_x

        def piece(a):
            return WA.at[zs, y, a % 4, c, :, cols] if half == 0 else WA.at[zs, a % 4, x, c, :, cols]

        def block(b, lo=0, n=4):
            if half == 0:
                return WA.at[zs, b % 4, pl.ds(lo, n), c, :, cols]
            return WA.at[zs, pl.ds(lo, n), b % 4, c, :, cols]

        ks = together(WA.at[0, 0, pl.ds(0, 3), 0, :, cols])
        p = piece(me1)
        up = send(p, p, ax1(1), ks)
        down = send(p, p, ax1(3), ks)
        yield
        up.wait_recv()
        p = piece(me1 + 3)
        far = send(p, p, ax1(1), ks)
        down.wait_recv()
        yield
        far.wait_recv()
        ks = together(go_tw.at[pl.ds(0, 224)])
        b = block(me2)
        up = send(b, b, ax2(1), ks)
        down = send(b, b, ax2(3), ks)
        tw, to_twin = group(WA.at[0, :, :, 0, :, cols], ks)
        to_twin(b, b, twin)
        yield
        up.wait_recv()
        b = block(me2 + 3, 0, 2)
        far_p = send(b, b, ax2(1), ks)
        b = block(me2 + 3)
        to_twin(b, b, twin)
        down.wait_recv()
        b = block(me2 + 1, 2, 2)
        far_m = send(b, b, ax2(3), ks)
        b = block(me2 + 1)
        to_twin(b, b, twin)
        yield
        far_p.wait_recv()
        far_m.wait_recv()
        b = block(me2 + 2)
        to_twin(b, b, twin)
        yield
        tw.wait_recv()
        yield

    def gather_z():
        own = WC.at[z, c, y]
        row_ks = take(1)
        row, to_row = group(own, row_ks)
        trio = WC.at[0, 0, pl.ds(0, 3)]

        def start_row():
            for d in (1, 2, 3):
                to_row(own, own, at_x(d))

        pl.when(source)(start_row)
        yield
        pl.when(jnp.logical_not(source))(row.wait_recv)
        col = send_group(trio, [(own, own, at_y(d)) for d in (2, 1, 3)])
        yield
        col.wait_recv()

        def block(d, lo=0, n=4):
            return WC.at[(z + d) % 8, c, pl.ds(lo, n)]

        b = block(0)
        ks = together(go_tw.at[pl.ds(0, 448)])
        up, down = send(b, b, at_z(1), ks), send(b, b, at_z(7), ks)
        tw, to_twin = group(WC.at[:, 0])
        to_twin(b, b, twin)
        yield
        for step in (1, 2, 3):
            n = 2 if step == 3 else 4
            up.wait_recv()
            b = block(8 - step, 0, n)
            up = send(b, b, at_z(1), ks)
            down.wait_recv()
            b = block(step, 4 - n, n)
            down = send(b, b, at_z(7), ks)
            for d in (8 - step, step):
                b = block(d)
                to_twin(b, b, twin)
            yield
        up.wait_recv()
        down.wait_recv()
        b = block(4)
        to_twin(b, b, twin)
        yield
        tw.wait_recv()
        pl.when(source)(copy(trio, trio, twin, 0, row_ks).wait_send)
        yield

    def scatter(h):
        if h == 0:
            me1, me2, ax1, ax2 = x, y, at_x, at_y
        else:
            me1, me2, ax1, ax2 = y, x, at_y, at_x

        def piece(buf, a, s, b):
            return buf.at[a % 4, s, b % 4, 0] if h == 0 else buf.at[b % 4, s, a % 4, 1]

        ks = together(go_tw.at[pl.ds(0, 496)])
        turn = (2, 1, 3, 0)
        far, near, both = {}, {}, {}

        def send_far(p):
            far[p] = [
                send_group(
                    R2.at[h, j, pl.ds(2 * p, 2)],
                    [(piece(Gs, me1 + 2, j, me2 + turn[q]), R2.at[h, j, q], to) for q in (2 * p, 2 * p + 1)],
                    ks,
                )
                for j, to in enumerate((ax1(1), ax1(3)))
            ]

        def send_near(p):
            near[p] = [
                send_group(
                    R1.at[h, j, 1 - j, pl.ds(2 * p, 2)],
                    [(piece(Gs, a, 1 - j, me2 + turn[q]), R1.at[h, j, 1 - j, q], to) for q in (2 * p, 2 * p + 1)],
                    ks,
                )
                for j, (a, to) in enumerate(((me1 + 1, ax1(1)), (me1 + 3, ax1(3))))
            ]

        def send_both(p):
            both[p] = []
            for j, (a, to) in enumerate(((me1 + 1, ax1(1)), (me1 + 3, ax1(3)))):
                far[p][j].wait_recv()
                copies = []
                for q in (2 * p, 2 * p + 1):
                    b = me2 + turn[q]
                    r = piece(Gs, a, j, b)
                    r[...] = (piece(G, a, j, b)[...] + R2[h, j, q].astype(F32)).astype(BF16)
                    copies.append((r, R1.at[h, j, j, q], to))
                both[p].append(send_group(R1.at[h, j, j, pl.ds(2 * p, 2)], copies, ks))

        def arrived(p):
            for cp in (*near[p], *both[p]):
                cp.wait_recv()

        def total(q):
            b = me2 + turn[q]
            for s in range(2):
                g = piece(G, me1, s, b)
                v = g[...] + R1[h, 0, s, q].astype(F32) + R1[h, 1, s, q].astype(F32)
                g[...] = v
                piece(Gs, me1, s, b)[...] = v.astype(BF16)

        def two(buf, q, s):
            return piece(buf, me1, s, me2 + turn[q])

        send_far(0)
        yield
        send_far(1)
        yield
        send_near(0)
        yield
        send_both(0)
        yield
        send_near(1)
        yield
        send_both(1)
        yield
        arrived(0)
        total(0)
        far_p = send(two(Gs, 0, 0), Q2.at[h, 0], ax2(1), ks)
        far_m = send(two(Gs, 0, 1), Q2.at[h, 1], ax2(3), ks)
        total(1)
        near_p = send(two(Gs, 1, 1), Q1.at[h, 0, 1], ax2(1), ks)
        yield
        far_p.wait_recv()
        two(Gs, 1, 0)[...] = (two(G, 1, 0)[...] + Q2[h, 0].astype(F32)).astype(BF16)
        both_p = send(two(Gs, 1, 0), Q1.at[h, 0, 0], ax2(1), ks)
        yield
        arrived(1)
        total(2)
        near_m = send(two(Gs, 2, 0), Q1.at[h, 1, 0], ax2(3), ks)
        far_m.wait_recv()
        two(Gs, 2, 1)[...] = (two(G, 2, 1)[...] + Q2[h, 1].astype(F32)).astype(BF16)
        both_m = send(two(Gs, 2, 1), Q1.at[h, 1, 1], ax2(3), ks)
        total(3)
        yield
        for cp in (near_p, near_m, both_p, both_m):
            cp.wait_recv()
        away = 1 - zh
        two(Gs, 3, away)[...] = (
            two(G, 3, away)[...] + Q1[h, 0, away].astype(F32) + Q1[h, 1, away].astype(F32)
        ).astype(BF16)
        last = send(two(Gs, 3, away), Z3.at[h], at_z(4), ks)
        yield
        mine = two(G, 3, zh)[...] + Q1[h, 0, zh].astype(F32) + Q1[h, 1, zh].astype(F32)
        last.wait_recv()
        res[pl.ds(16 * h, 16), :] = mine + Z3[h].astype(F32)
        yield

    def allreduce(k):
        cp = send(T.at[k, 1 - c], RC.at[k], twin)
        yield
        cp.wait_recv()
        v = T[k, c] + RC[k]
        A1[k] = jnp.concatenate([v[..., :256], v[..., 256:]], axis=2).astype(BF16)
        got = send_group(
            RP.at[k],
            [
                (A1.at[k, (x + dx) % 4, (y + dy) % 4], RP.at[k, e], at_xy(dx, dy))
                for e, (dx, dy) in enumerate(plane)
            ],
        )
        yield
        got.wait_recv()
        v = RP[k, 0].astype(F32)
        for e in range(1, len(plane)):
            v = v + RP[k, e].astype(F32)
        v = T[k, c, x, y] + RC[k, x, y] + jnp.concatenate([v[:8], v[8:]], axis=1)
        mine = RZ.at[k, z]
        mine[...] = v
        got = send_group(RZ.at[k, pl.ds(0, 7)], [(mine, mine, at_z(d)) for d in (4, 3, 5, 2, 6, 1, 7)])
        yield
        got.wait_recv()
        v = ((RZ[k, 0] + RZ[k, 1]) + (RZ[k, 2] + RZ[k, 3])) + ((RZ[k, 4] + RZ[k, 5]) + (RZ[k, 6] + RZ[k, 7]))
        mine = F.at[k, c * 4 + x, y]
        mine[...] = v
        got = send_group(RP2, [(mine, mine, at_xy(*p)) for p in plane])
        yield
        got.wait_recv()
        half = F.at[k, pl.ds(c * 4, 4)]
        cp = send(half, half, twin)
        yield
        cp.wait_recv()
        yield

    def full(k):
        return jnp.concatenate([F[k, :, j].reshape(R, 512) for j in range(4)], axis=1)

    def put(k, v):
        for a in range(8):
            for j in range(4):
                T[k, a // 4, a % 4, j] = v[8 * a : 8 * (a + 1), 512 * j : 512 * (j + 1)]

    def my_rows(k):
        v = F[k, :, i // 16].reshape(R, 512)
        for n in (128, 32):
            place = (i // (n // 32)) % 4
            blk = v[:, :n]
            for j in range(1, 4):
                blk = jnp.where(place == j, v[:, n * j : n * (j + 1)], blk)
            v = blk
        return v

    own_w = [gather(True, h) for h in range(2)]
    oth_w = [gather(False, h) for h in range(2)]
    z_w = gather_z()
    grads = [scatter(h) for h in range(2)]
    red = [allreduce(k) for k in range(2)]

    def adv(*gens):
        for g in gens:
            next(g)

    def transpose_acts():
        for b in range(8):
            t = acts[:, 256 * b : 256 * (b + 1)].T
            for j in range(8):
                AT[j % 2, j // 2, pl.ds(32 * b, 32)] = t[32 * j : 32 * (j + 1)]

    def error_term(b3):
        eb = fold3(nt(b3, split3(err[...])))
        eb = jnp.concatenate([eb[:, :32] + (eb[:, 32:64] + eb[:, 64:])] * 4, axis=1)
        col = lax.broadcasted_iota(jnp.int32, (R, D), 1)
        return jnp.where(col // 32 == i, jnp.concatenate([eb] * 16, axis=1), 0.0)

    def left_factor(b3, eb):
        u = fold3(nt(b3, go[...]))
        al.wait()
        p = fold3(nn(split3(u), acts[...]))
        put(0, (p * scale + eb) * (1.0 / GROUPS))

    def right_factor():
        pt = full(0)
        v = fold3(nt(split3(pt), acts[...]))
        s = fold3(nn(split3(v), go[...]))
        pe = nn(my_rows(0), err[...], HI)
        put(1, (s * scale + pe) * (1.0 / GROUPS))

    def gram():
        pt = full(0)
        row = lax.broadcasted_iota(jnp.int32, (R, R), 0)
        col = lax.broadcasted_iota(jnp.int32, (R, R), 1)
        M[...] = jnp.concatenate([nt(pt, pt, HI), (row == col).astype(F32)], axis=1)

    def factor(lo, hi):
        row = lax.broadcasted_iota(jnp.int32, (R, 2 * R), 0)
        col = lax.broadcasted_iota(jnp.int32, (R, 2 * R), 1)

        def body(k, m):
            rk = jnp.sum(jnp.where(row == k, m, 0.0), axis=0, keepdims=True)
            ck = jnp.sum(jnp.where(col == k, m, 0.0), axis=1, keepdims=True)
            piv = jnp.sum(jnp.where(col[:1] == k, rk, 0.0), axis=1, keepdims=True)
            rk = rk / jnp.sqrt(piv)
            ck = ck / jnp.sqrt(piv)
            return jnp.where(row > k, m - ck * rk, jnp.where(row == k, rk, m))

        M[...] = lax.fori_loop(lo, hi, body, M[...])

    def grad_own(d):
        a = (x + d) % 4

        def body(n, carry):
            cols = pl.ds(pl.multiple_of(n * 512, 512), 512)
            v = nn(AT[c, a], go[:, cols])
            G[a, :, :, :, :, cols] = v.reshape(2, 4, 2, 16, 512)
            return carry

        lax.fori_loop(0, 4, body, 0)

    def grad_twin(d):
        a = (x + d) % 4

        def body(n, carry):
            cols = pl.ds(pl.multiple_of(n * 512, 512), 512)
            v = nn(RT[a], go_tw[:, cols]).reshape(2, 4, 2, 16, 512)
            v = (v + G[a, :, :, :, :, cols]) * scale
            G[a, :, :, :, :, cols] = v
            Gs[a, :, :, :, :, cols] = v.astype(BF16)
            return carry

        lax.fori_loop(0, 4, body, 0)

    def grad_acts(s, *blocks):
        for b in blocks:
            w = jnp.concatenate(
                [v for a in range(4) for k in range(2) for v in (WA[s, b, a, k], WC[s * 4 + (a + b) % 4, k, b])], axis=0
            )
            cols = pl.ds(pl.multiple_of((s * 4 + b) * 256, 256), 256)
            ga[:, cols] = nt(go[...], w).astype(BF16)

    def drain():
        while sent:
            sent.pop(0).wait_send()

    wl[0].wait()
    bl.wait()
    b3 = split3(basis[...])
    el.wait()
    eb = error_term(b3)
    pl.when(source)(wl[1].wait)
    pl.semaphore_wait(barrier, len(peers))
    adv(*own_w)
    wz = send(WA.at[zh, y, x, c], WA.at[zh, y, x, c], mirror)
    adv(z_w)
    gl.wait()
    left_factor(b3, eb)
    adv(red[0])
    got = [send(go, go_tw, twin)]
    transpose_acts()
    got.append(send(AT.at[1 - c], RT, twin))
    adv(red[0])
    adv(*own_w)
    adv(z_w)
    grad_own(2)
    grad_own(1)
    adv(red[0])
    wz.wait_recv()
    adv(*oth_w)
    grad_own(3)
    adv(*own_w)
    adv(z_w)
    grad_own(0)
    adv(*oth_w)
    for cp in got:
        cp.wait_recv()
    grad_twin(2)
    adv(red[0])
    adv(*own_w)
    adv(grads[0])
    adv(grads[0])
    grad_twin(1)
    grad_twin(3)
    adv(grads[0])
    grad_twin(0)
    adv(grads[1])
    adv(grads[1])
    adv(grads[1])
    adv(red[0])
    adv(z_w)
    adv(red[0])
    right_factor()
    adv(red[1])
    gram()
    adv(red[1])
    adv(*grads)
    adv(*grads)
    factor(0, 16)
    adv(z_w)
    adv(*grads)
    factor(16, 32)
    adv(red[1])
    adv(*grads)
    adv(*oth_w)
    adv(*own_w)
    factor(32, 48)
    adv(*own_w)
    adv(z_w)
    adv(red[1])
    factor(48, 64)
    ortho = nn(M[:, R:], my_rows(0), HI).T
    adv(*grads)
    adv(*grads)
    adv(z_w)
    adv(z_w)
    grad_acts(zh, 0, 1, 2, 3)
    adv(*oth_w)
    adv(red[1])
    adv(*grads)
    adv(red[1])
    qf = nn(M[:, R:], full(1), HI)
    qt[...] = qf
    ap = nn(ortho, qf, HI)
    apv[...] = ap
    adv(*oth_w)
    adv(*oth_w)
    grad_acts(1 - zh, 0, 1, 2, 3)
    adv(*grads)
    res[...] = res[...] + err[...] - ap
    drain()
    assert count[0] == RECV and count[1] == SEND, count
    for g in own_w + oth_w + [z_w] + grads + red:
        assert next(g, 0) == 0


def write_out(a, b, c, d, ao, bo, co, do, sem):
    cps = [pltpu.make_async_copy(v, o, sem.at[k]) for k, (v, o) in enumerate(((a, ao), (b, bo), (c, co), (d, do)))]
    for cp in cps:
        cp.start()
    for cp in cps:
        cp.wait()


def shards(acts, grad_out, weight, error, basis):
    scale = 1.0 / math.sqrt(TOK * lax.axis_size("inner"))
    hbm = pl.BlockSpec(memory_space=pltpu.HBM)
    vm = pltpu.VMEM
    ga, approx, err, qt = pl.pallas_call(
        functools.partial(kernel, scale),
        out_shape=(vm((TOK, D), BF16), vm((32, D), F32), vm((32, D), F32), vm((R, D), F32)),
        in_specs=[hbm] * 5,
        out_specs=(pl.BlockSpec(memory_space=vm),) * 4,
        scratch_shapes=[
            vm((TOK, D), BF16),
            vm((TOK, D), BF16),
            vm((32, D), F32),
            vm((R, D), F32),
            vm((2, 4, 4, 2, 16, D), BF16),
            vm((8, 2, 4, 16, D), BF16),
            vm((2, 4, 256, TOK), BF16),
            vm((4, 256, TOK), BF16),
            vm((TOK, D), BF16),
            vm((4, 2, 4, 2, 16, D), F32),
            vm((4, 2, 4, 2, 16, D), BF16),
            vm((2, 2, 2, 4, 16, D), BF16),
            vm((2, 2, 4, 16, D), BF16),
            vm((2, 2, 2, 16, D), BF16),
            vm((2, 2, 16, D), BF16),
            vm((2, 16, D), BF16),
            vm((2, 2, 4, 4, 8, 512), F32),
            vm((2, 4, 4, 8, 512), F32),
            vm((2, 4, 4, 16, 256), BF16),
            vm((2, 15, 16, 256), BF16),
            vm((15, 8, 512), F32),
            vm((2, 8, 8, 512), F32),
            vm((2, 8, 4, 8, 512), F32),
            vm((R, 2 * R), F32),
            pltpu.SemaphoreType.DMA((6,)),
            pltpu.SemaphoreType.DMA((SEND,)),
            pltpu.SemaphoreType.DMA((RECV,)),
        ],
        compiler_params=pltpu.CompilerParams(
            collective_id=0, has_side_effects=True, vmem_limit_bytes=60 * 2**20
        ),
        name="powersgd",
    )(acts, grad_out, weight, error[0], basis.T)
    ga, approx, err, qt = pl.pallas_call(
        write_out,
        out_shape=(
            jax.ShapeDtypeStruct((TOK, D), BF16),
            jax.ShapeDtypeStruct((32, D), F32),
            jax.ShapeDtypeStruct((32, D), F32),
            jax.ShapeDtypeStruct((R, D), F32),
        ),
        in_specs=[pl.BlockSpec(memory_space=pl.ANY)] * 4,
        out_specs=(hbm,) * 4,
        scratch_shapes=[pltpu.SemaphoreType.DMA((4,))],
        compiler_params=pltpu.CompilerParams(vmem_limit_bytes=2**20),
        name="write_out",
    )(ga, approx, err, qt)
    return (ga, approx, err[None], qt.T)


def solution(mesh):
    in_specs = (
        P(("inner", "outer"), None),
        P(("inner", "outer"), None),
        P("inner", None),
        P("outer", "inner", None),
        P(),
    )
    out_specs = (P(("inner", "outer"), None), P("inner", None), P("outer", "inner", None), P())
    return jax.shard_map(shards, mesh=mesh, in_specs=in_specs, out_specs=out_specs, check_vma=False)
```
